256 devices in a mesh: anc: 32 (over x, y, core), cand: 8 (over z).
Axes of the slice: x: 4, y: 4, z: 8, core: 2. Of those that a mesh axis runs over, the one named last changes fastest.
Arguments:
- anchors: float32 [32768, 256], P('anc'), may hold values from -300 to 300
- candidates: float32 [32768, 256], P('cand'), may hold values from -20 to 20
- positives: int32 [32768], P('anc'), may hold values from 0 to 32767
Outputs:
- mean_loss: float32 [], replicated
- anchor_grad: float32 [32768, 256], P(('anc', 'cand'))
- cand_grad: float32 [8, 4096, 256], P('cand', 'anc')
The draws below stay inside these ranges and needn't reach their ends.
All inputs are finite; a program needn't handle non-finite values.
Results may differ from the reference program's by a relative error of at most 0.0003.
Values sent between devices are 32-bit elements; how exact they have to be, the bound alone decides.
A program may use at most 128 MiB of HBM per device.

```python
import math
import jax
import jax.numpy as jnp
from jax import lax

E = 256
CAND_DEV = 4096
NUM_ANCHORS = 32768
NUM_CANDS = 32768
N_CAND = 8


def base_rows(key):
    return jax.random.normal(key, (NUM_CANDS, E), jnp.float32)


def draw_candidates(key, part):
    base = base_rows(key)
    key = jax.random.fold_in(key, 7)
    scales = jnp.exp(jax.random.uniform(key, (NUM_CANDS, 1), jnp.float32, math.log(0.3), math.log(3.0)))
    values = base * scales
    return jnp.clip(values, -20.0, 20.0)


def draw_anchors(key, part):
    base = base_rows(key)
    key = jax.random.fold_in(key, 3)
    first, second, third = jax.random.split(key, 3)
    position = jnp.arange(NUM_ANCHORS, dtype=jnp.int32)
    rising = 1.0 + 2.0 * position.astype(jnp.float32) / NUM_ANCHORS
    scales = jnp.exp(jax.random.uniform(second, (NUM_ANCHORS, 1), jnp.float32, math.log(0.5), math.log(2.0))) * rising[:, None]
    raw = jax.random.normal(first, (NUM_ANCHORS, E), jnp.float32)
    values = raw * scales
    picks = jax.random.randint(third, (NUM_ANCHORS, 2), 0, NUM_CANDS)
    aligned = 0.5 * (base[picks[:, 0]] + base[picks[:, 1]])
    strength = 30.0 * (1.0 + (position % 4).astype(jnp.float32))
    strong = position % 16 == 0
    values = jnp.where(strong[:, None], aligned * strength[:, None], values)
    return jnp.clip(values, -300.0, 300.0)


def place_ends(values, rng, least, high):
    longest = values.shape.index(max(values.shape))
    spots = []
    for shift in (0, 1):
        where = [jax.random.randint(jax.random.fold_in(rng, axis), (), 0, length) for axis, length in enumerate(values.shape)]
        where[longest] = (where[longest] + shift) % values.shape[longest]
        spots.append(tuple(where))
    return values.at[spots[0]].set(least).at[spots[1]].set(high)


def setup_inputs(seed: int = 0) -> dict:
    streams_of = jax.random.split(jax.random.key(seed), 4)
    return {
        "anchors": draw_anchors(jax.random.fold_in(streams_of[3], 71), 0),
        "candidates": draw_candidates(jax.random.fold_in(streams_of[3], 71), 0),
        "positives": place_ends(jax.random.randint(streams_of[2], (NUM_ANCHORS,), 0, NUM_CANDS), jax.random.fold_in(streams_of[2], 1), 0, NUM_CANDS - 1).astype(jnp.int32),
    }


def reference(anchors, candidates, positives):
    scale = 0.25 / math.sqrt(E)
    block = math.gcd(NUM_ANCHORS, 512)
    count = NUM_ANCHORS // block
    columns = jnp.arange(NUM_CANDS, dtype=jnp.int32)

    def one_block(carry, index):
        start = (index * block).astype(jnp.int32)
        rows = lax.dynamic_slice_in_dim(anchors, start, block, 0)
        picks = lax.dynamic_slice_in_dim(positives, start, block, 0)
        logits = jnp.dot(rows, candidates.T, precision=lax.Precision.HIGHEST, preferred_element_type=jnp.float32) * scale
        row_max = lax.optimization_barrier(jnp.max(logits, axis=1))
        total = lax.optimization_barrier(jnp.sum(jnp.exp(logits - row_max[:, None]), axis=1))
        lse = row_max + jnp.log(total)
        hit = columns[None, :] == picks[:, None]
        positive_logit = lax.optimization_barrier(jnp.sum(jnp.where(hit, logits, jnp.zeros_like(logits)), axis=1))
        weights = jnp.exp(logits - lse[:, None]) - hit.astype(logits.dtype)
        anchor_part = jnp.dot(weights, candidates, precision=lax.Precision.HIGHEST, preferred_element_type=jnp.float32) * scale
        carry = carry + jnp.dot(weights.T, rows, precision=lax.Precision.HIGHEST, preferred_element_type=jnp.float32) * scale
        return (carry, (anchor_part, jnp.sum(lse - positive_logit)))
    start_grad = jnp.zeros((NUM_CANDS, E), jnp.float32)
    cand_total, (anchor_parts, losses) = lax.scan(one_block, start_grad, jnp.arange(count, dtype=jnp.int32))
    mean_loss = jnp.sum(losses) / NUM_ANCHORS
    anchor_grad = anchor_parts.reshape(NUM_ANCHORS, E)
    cand_grad = cand_total.reshape(N_CAND, CAND_DEV, E)
    return (mean_loss, anchor_grad, cand_grad)
```

```python
import math

import jax
import jax.numpy as jnp
from jax import lax
from jax.experimental import pallas as pl
from jax.experimental.pallas import tpu as pltpu
from jax.sharding import PartitionSpec as P

F32 = jnp.float32
BF16 = jnp.bfloat16
WIDTH = 256
ANCHORS = 1024
CANDS = 4096
TILE = 512
TILES = CANDS // TILE
LOG2E = math.log2(math.e)
LN2 = math.log(2.0)
SCALE = 0.25 / math.sqrt(WIDTH)
SLABS = (2, 1, 3, 0)
PAIRS = ((4, 3), (5, 2), (6, 1), (7, 0))


def split(value):
    high = value.astype(BF16)
    return high, (value - high.astype(F32)).astype(BF16)


def dot(left, right):
    return jnp.dot(left, right, preferred_element_type=F32)


def dot_nt(left, right):
    return lax.dot_general(left, right, (((1,), (1,)), ((), ())), preferred_element_type=F32)


class Copies:
    def __init__(self, send_sems, recv_sems):
        self.send_sems, self.recv_sems = send_sems, recv_sems
        self.made = []

    def start(self, source, target, device):
        index = len(self.made)
        copy = pltpu.make_async_remote_copy(
            src_ref=source,
            dst_ref=target,
            send_sem=self.send_sems.at[index],
            recv_sem=self.recv_sems.at[index],
            device_id=device,
            device_id_type=pl.DeviceIdType.MESH,
        )
        copy.start()
        self.made.append(copy)
        return copy


def kernel(
    a_ref, c_ref, pos_ref, loss_ref, agrad_ref, cgrad_ref,
    c_hi, c_lo, ct_hi, ct_lo, al_hi, al_lo, as_hi, as_lo,
    p_ref, w_hi, w_lo, stat, back, stat_rx, loss_rx,
    slab, pair_rx, q0, q1, x0, y1, rx0, rx1, ry0, ry1, grad, z_rx,
    send_sems, recv_sems,
):
    anc = lax.axis_index("anc")
    z = lax.axis_index("cand")
    x, y, core = anc // 8, lax.rem(anc // 2, 4), lax.rem(anc, 2)

    def at(dx=0, dy=0, other=False, dz=0):
        px = lax.rem(x + dx, 4)
        py = lax.rem(y + dy, 4)
        pc = 1 - core if other else core
        return ((px * 4 + py) * 2 + pc, lax.rem(z + dz, 8))

    peers = [at(other=True)]
    peers += [at(dx=d) for d in (1, 2, 3)] + [at(dy=d) for d in (1, 2, 3)]
    peers += [at(dz=d) for d in range(1, 8)]
    barrier = pltpu.get_barrier_semaphore()
    for peer in peers:
        pl.semaphore_signal(barrier, inc=1, device_id=peer, device_id_type=pl.DeviceIdType.MESH)

    copies = Copies(send_sems, recv_sems)
    rows_iota = lax.broadcasted_iota(jnp.int32, (TILE, 1), 0)

    al_hi[...], al_lo[...] = split(a_ref[...] * (SCALE * LOG2E))
    as_hi[...], as_lo[...] = split(a_ref[...] * SCALE)

    @pl.loop(0, TILES)
    def _(j):
        rows = pl.ds(pl.multiple_of(j * TILE, TILE), TILE)
        block = c_ref[rows, :]
        ch, cl = split(block)
        c_hi[rows, :], c_lo[rows, :] = ch, cl
        th, tl = split((block * SCALE).T)
        ct_hi[j], ct_lo[j] = th, tl
        left = jnp.concatenate([ch, cl, ch], axis=1)
        first = z * CANDS + j * TILE
        for i in range(4):
            lanes = slice(i * 256, (i + 1) * 256)
            ah, al = al_hi[lanes, :], al_lo[lanes, :]
            logits = dot_nt(left, jnp.concatenate([ah, ah, al], axis=1))
            hit = rows_iota == pos_ref[0:1, lanes] - first
            top = jnp.max(logits, axis=0, keepdims=True)
            stat[j, 2:3, lanes] = jnp.sum(jnp.where(hit, logits, 0.0), axis=0, keepdims=True)
            prob = jnp.exp2(logits - top)
            stat[j, 0:1, lanes] = top
            stat[j, 1:2, lanes] = jnp.sum(prob, axis=0, keepdims=True)
            p_ref[rows, lanes] = prob

    tops = [stat[j, 0:1, :] for j in range(TILES)]
    top = tops[0]
    for j in range(1, TILES):
        top = jnp.maximum(top, tops[j])
    total = jnp.zeros_like(top)
    chosen = jnp.zeros_like(top)
    for j in range(TILES):
        total += stat[j, 1:2, :] * jnp.exp2(tops[j] - top)
        chosen += stat[j, 2:3, :]
    for k in range(8):
        lanes = slice(k * 128, (k + 1) * 128)
        stat_rx[z, 0, k:k + 1, :] = top[:, lanes]
        stat_rx[z, 1, k:k + 1, :] = total[:, lanes]
        stat_rx[z, 2, k:k + 1, :] = chosen[:, lanes]

    pl.semaphore_wait(barrier, len(peers))
    sent = [copies.start(stat_rx.at[z], stat_rx.at[z], at(dz=d)) for d in range(1, 8)]
    for copy in sent:
        copy.wait_recv()
    top = stat_rx[0, 0]
    for k in range(1, 8):
        top = jnp.maximum(top, stat_rx[k, 0])
    total = jnp.zeros_like(top)
    chosen = jnp.zeros_like(top)
    for k in range(8):
        total += stat_rx[k, 1] * jnp.exp2(stat_rx[k, 0] - top)
        chosen += stat_rx[k, 2]
    lse = top + jnp.log2(total)
    loss_rx[0, core] = (lse - chosen) * LN2
    loss_copy = copies.start(loss_rx.at[0, core], loss_rx.at[0, core], at(other=True))
    lse_row = jnp.concatenate([lse[k:k + 1, :] for k in range(8)], axis=1)
    for j in range(TILES):
        back[j] = jnp.exp2(stat[j, 0:1, :] - lse_row)

    def cand_slab(s):
        px = lax.rem(x + SLABS[s], 4)

        @pl.loop(0, 2)
        def _(half):
            j = px * 2 + half
            rows = pl.ds(pl.multiple_of(j * TILE, TILE), TILE)
            first = z * CANDS + j * TILE
            highs, lows = [], []
            for k in range(8):
                lanes = slice(k * 128, (k + 1) * 128)
                weight = p_ref[rows, lanes] * back[j, :, lanes]
                hit = rows_iota == pos_ref[0:1, lanes] - first
                wh, wl = split(jnp.where(hit, weight - 1.0, weight))
                w_hi[k, rows, :], w_lo[k, rows, :] = wh, wl
                highs.append(wh)
                lows.append(wl)
            wh, wl = jnp.concatenate(highs, axis=1), jnp.concatenate(lows, axis=1)
            part = dot(wh, as_hi[...]) + dot(wl, as_hi[...]) + dot(wh, as_lo[...])
            for q in range(4):
                slab[s, half * 2 + q // 2, q % 2] = part[q * 128:(q + 1) * 128, :]

        return copies.start(slab.at[s, :, 1 - core], pair_rx.at[s], at(other=True))

    def pair_sum(s, copy):
        copy.wait_recv()
        for dy in range(4):
            py = lax.rem(y + dy, 4)
            both = slab[s, py, core] + pair_rx[s, py]
            q0[s, dy] = both[:, :128]
            q1[dy, s] = both[:, 128:]

    def anchor_pair(pair):
        places = [lax.rem(z + d, 8) for d in pair]
        acc = None
        for j in range(TILES):
            rows = slice(j * TILE, (j + 1) * TILE)
            wh = jnp.concatenate([w_hi[p, rows, :] for p in places], axis=1)
            wl = jnp.concatenate([w_lo[p, rows, :] for p in places], axis=1)
            part = dot(ct_hi[j], wh) + dot(ct_lo[j], wh) + dot(ct_hi[j], wl)
            acc = part if acc is None else acc + part
        for n, d in enumerate(pair):
            for h in range(2):
                grad[d, h] = acc[h * 128:(h + 1) * 128, n * 128:(n + 1) * 128]

    z_right, z_left = {}, {}

    def send_right(d, h):
        slot = len(z_right) + len(z_left)
        z_right[d - 1, h] = (slot, copies.start(grad.at[d, h], z_rx.at[slot], at(dz=1)))

    def send_left(d, h):
        slot = len(z_right) + len(z_left)
        z_left[(d + 1) % 8, h] = (slot, copies.start(grad.at[d, h], z_rx.at[slot], at(dz=7)))

    def add_to(side, d, h):
        slot, copy = side[d, h]
        copy.wait_recv()
        grad[d, h] = grad[d, h] + z_rx[slot]

    def pass_right(d, h):
        add_to(z_right, d, h)
        send_right(d, h)

    def pass_left(d, h):
        add_to(z_left, d, h)
        send_left(d, h)

    right_x, left_x, right_y, left_y = at(dx=1), at(dx=3), at(dy=1), at(dy=3)

    pair0 = cand_slab(0)
    loss_copy.wait_recv()
    loss_rx[1, x] = loss_rx[0, 0] + loss_rx[0, 1]
    loss_copies = [copies.start(loss_rx.at[1, x], loss_rx.at[1, x], at(dx=d)) for d in (1, 2, 3)]

    pair1 = cand_slab(1)
    pair_sum(0, pair0)
    x_far_r = copies.start(q0.at[0, 0:2], rx0.at[0], right_x)
    x_far_l = copies.start(q0.at[0, 2:4], rx0.at[1], left_x)
    for copy in loss_copies:
        copy.wait_recv()
    loss_rx[2, y] = (loss_rx[1, 0] + loss_rx[1, 1]) + (loss_rx[1, 2] + loss_rx[1, 3])
    loss_copies = [copies.start(loss_rx.at[2, y], loss_rx.at[2, y], at(dy=d)) for d in (1, 2, 3)]

    pair2 = cand_slab(2)
    pair_sum(1, pair1)
    x_near = [copies.start(q0.at[1, 2:4], rx0.at[2], right_x)]
    y_far_r = copies.start(q1.at[2, 0:2], ry1.at[0], right_y)
    y_near = [copies.start(q1.at[3, 0:2], ry1.at[1], left_y)]
    x_far_r.wait_recv()
    q0[1, 0:2] = q0[1, 0:2] + rx0[0]
    x_near.append(copies.start(q0.at[1, 0:2], rx0.at[3], right_x))

    pair3 = cand_slab(3)
    pair_sum(2, pair2)
    x_near.append(copies.start(q0.at[2, 0:2], rx0.at[4], left_x))
    x_far_l.wait_recv()
    q0[2, 2:4] = q0[2, 2:4] + rx0[1]
    x_near.append(copies.start(q0.at[2, 2:4], rx0.at[5], left_x))
    y_far_r.wait_recv()
    q1[1, 0:2] = q1[1, 0:2] + ry1[0]
    y_near.append(copies.start(q1.at[1, 0:2], ry1.at[2], right_y))
    for copy in loss_copies:
        copy.wait_recv()
    losses = (loss_rx[2, 0] + loss_rx[2, 1]) + (loss_rx[2, 2] + loss_rx[2, 3])
    loss_ref[...] = jnp.sum(losses, keepdims=True) * (1.0 / (32 * ANCHORS))

    anchor_pair(PAIRS[0])
    send_right(4, 0)
    send_left(4, 1)
    send_right(3, 1)
    pair_sum(3, pair3)
    y_far_l = copies.start(q1.at[2, 2:4], ry1.at[3], left_y)
    y_near.append(copies.start(q1.at[1, 2:4], ry1.at[4], right_y))
    for copy in x_near:
        copy.wait_recv()
    x0[0:2] = q0[3, 0:2] + rx0[3] + rx0[4]
    x0[2:4] = q0[3, 2:4] + rx0[2] + rx0[5]
    f_far_r = copies.start(x0.at[2, 0:64], ry0.at[0], right_y)
    f_far_l = copies.start(x0.at[2, 64:128], ry0.at[1], left_y)
    f_near = [
        copies.start(x0.at[1, 64:128], ry0.at[2], right_y),
        copies.start(x0.at[3, 0:64], ry0.at[3], left_y),
    ]

    anchor_pair(PAIRS[1])
    send_left(5, 0)
    pass_right(3, 0)
    pass_right(2, 1)
    pass_left(5, 1)
    y_far_l.wait_recv()
    q1[3, 2:4] = q1[3, 2:4] + ry1[3]
    y_near.append(copies.start(q1.at[3, 2:4], ry1.at[5], left_y))
    f_far_r.wait_recv()
    x0[1, 0:64] = x0[1, 0:64] + ry0[0]
    f_near.append(copies.start(x0.at[1, 0:64], ry0.at[4], right_y))
    f_far_l.wait_recv()
    x0[3, 64:128] = x0[3, 64:128] + ry0[1]
    f_near.append(copies.start(x0.at[3, 64:128], ry0.at[5], left_y))

    anchor_pair(PAIRS[2])
    pass_right(2, 0)
    pass_right(1, 1)
    pass_left(6, 0)
    pass_left(6, 1)
    for copy in y_near:
        copy.wait_recv()
    y1[0:2] = q1[0, 0:2] + ry1[1] + ry1[2]
    y1[2:4] = q1[0, 2:4] + ry1[4] + ry1[5]
    s_far_r = copies.start(y1.at[0, 0:64], rx1.at[0], right_x)
    s_far_l = copies.start(y1.at[0, 64:128], rx1.at[1], left_x)
    s_near = [
        copies.start(y1.at[1, 64:128], rx1.at[2], right_x),
        copies.start(y1.at[2, 0:64], rx1.at[3], left_x),
    ]
    for copy in f_near:
        copy.wait_recv()
    cgrad_ref[0:64, 0:128] = x0[0, 0:64] + ry0[4] + ry0[3]
    cgrad_ref[64:128, 0:128] = x0[0, 64:128] + ry0[2] + ry0[5]

    anchor_pair(PAIRS[3])
    pass_right(1, 0)
    pass_left(7, 0)
    pass_left(7, 1)
    s_far_r.wait_recv()
    y1[1, 0:64] = y1[1, 0:64] + rx1[0]
    s_near.append(copies.start(y1.at[1, 0:64], rx1.at[4], right_x))
    s_far_l.wait_recv()
    y1[2, 64:128] = y1[2, 64:128] + rx1[1]
    s_near.append(copies.start(y1.at[2, 64:128], rx1.at[5], left_x))

    for h in range(2):
        add_to(z_right, 0, h)
        add_to(z_left, 0, h)
        agrad_ref[:, h * 128:(h + 1) * 128] = grad[0, h].T
    for copy in s_near:
        copy.wait_recv()
    cgrad_ref[0:64, 128:256] = y1[3, 0:64] + rx1[4] + rx1[3]
    cgrad_ref[64:128, 128:256] = y1[3, 64:128] + rx1[2] + rx1[5]
    for copy in copies.made:
        copy.wait_send()


def body(anchors, candidates, positives):
    vmem = pl.BlockSpec(memory_space=pltpu.VMEM)
    sems = 64
    loss, anchor_grad, cand_grad = pl.pallas_call(
        kernel,
        out_shape=[
            jax.ShapeDtypeStruct((1, 1), F32),
            jax.ShapeDtypeStruct((128, WIDTH), F32),
            jax.ShapeDtypeStruct((128, WIDTH), F32),
        ],
        in_specs=[vmem] * 3,
        out_specs=[vmem] * 3,
        scratch_shapes=[
            pltpu.VMEM((CANDS, WIDTH), BF16),
            pltpu.VMEM((CANDS, WIDTH), BF16),
            pltpu.VMEM((TILES, WIDTH, TILE), BF16),
            pltpu.VMEM((TILES, WIDTH, TILE), BF16),
            pltpu.VMEM((ANCHORS, WIDTH), BF16),
            pltpu.VMEM((ANCHORS, WIDTH), BF16),
            pltpu.VMEM((ANCHORS, WIDTH), BF16),
            pltpu.VMEM((ANCHORS, WIDTH), BF16),
            pltpu.VMEM((CANDS, ANCHORS), F32),
            pltpu.VMEM((8, CANDS, 128), BF16),
            pltpu.VMEM((8, CANDS, 128), BF16),
            pltpu.VMEM((TILES, 8, ANCHORS), F32),
            pltpu.VMEM((TILES, 1, ANCHORS), F32),
            pltpu.VMEM((8, 3, 8, 128), F32),
            pltpu.VMEM((3, 4, 8, 128), F32),
            pltpu.VMEM((4, 4, 2, 128, WIDTH), F32),
            pltpu.VMEM((4, 4, 128, WIDTH), F32),
            pltpu.VMEM((4, 4, 128, 128), F32),
            pltpu.VMEM((4, 4, 128, 128), F32),
            pltpu.VMEM((4, 128, 128), F32),
            pltpu.VMEM((4, 128, 128), F32),
            pltpu.VMEM((6, 2, 128, 128), F32),
            pltpu.VMEM((6, 64, 128), F32),
            pltpu.VMEM((6, 64, 128), F32),
            pltpu.VMEM((6, 2, 128, 128), F32),
            pltpu.VMEM((8, 2, 128, 128), F32),
            pltpu.VMEM((14, 128, 128), F32),
            pltpu.SemaphoreType.DMA((sems,)),
            pltpu.SemaphoreType.DMA((sems,)),
        ],
        compiler_params=pltpu.CompilerParams(
            collective_id=0, has_side_effects=True, vmem_limit_bytes=63 << 20
        ),
    )(anchors, candidates, positives.reshape(1, ANCHORS))
    return (loss.reshape(()), anchor_grad, cand_grad[None])


def solution(mesh):
    in_specs = (P("anc", None), P("cand", None), P("anc"))
    out_specs = (P(), P(("anc", "cand"), None), P("cand", "anc", None))
    return jax.shard_map(body, mesh=mesh, in_specs=in_specs, out_specs=out_specs, check_vma=False)
```

```python
import math

import jax
import jax.numpy as jnp
from jax import lax
from jax.experimental import pallas as pl
from jax.experimental.pallas import tpu as pltpu
from jax.sharding import PartitionSpec as P

F32 = jnp.float32
BF16 = jnp.bfloat16
WIDTH = 256
ANCHORS = 1024
CANDS = 4096
TILE = 512
TILES = CANDS // TILE
LOG2E = math.log2(math.e)
LN2 = math.log(2.0)
SCALE = 0.25 / math.sqrt(WIDTH)
BLOCK = 256
AWAY = (2, 1, 3)


def split(value):
    high = value.astype(BF16)
    return high, (value - high.astype(F32)).astype(BF16)


def dot(left, right):
    return jnp.dot(left, right, preferred_element_type=F32)


def dot_nt(left, right):
    return lax.dot_general(left, right, (((1,), (1,)), ((), ())), preferred_element_type=F32)


class Copies:
    def __init__(self, send_sems, recv_sems):
        self.send_sems, self.recv_sems = send_sems, recv_sems
        self.made = []

    def start(self, source, target, device):
        index = len(self.made)
        copy = pltpu.make_async_remote_copy(
            src_ref=source,
            dst_ref=target,
            send_sem=self.send_sems.at[index],
            recv_sem=self.recv_sems.at[index],
            device_id=device,
            device_id_type=pl.DeviceIdType.MESH,
        )
        copy.start()
        self.made.append(copy)
        return copy


def kernel(
    a_hbm, c_hbm, pos_ref, loss_ref, agrad_ref, cgrad_ref,
    a_ref, c_ref, c_hi, c_lo, ct_hi, ct_lo, al_hi, al_lo, as_hi, as_lo,
    p_ref, w_hi, w_lo, stat, back, stat_rx, loss_rx,
    blocks, pair_rx, q0, q1, qa, qb, qo, rx0, ry1, from_y, from_x, grad, far_rx, z_rx,
    in_sems, send_sems, recv_sems,
):
    anc = lax.axis_index("anc")
    z = lax.axis_index("cand")
    x, y, core = anc // 8, lax.rem(anc // 2, 4), lax.rem(anc, 2)

    def at(dx=0, dy=0, other=False, dz=0):
        px = lax.rem(x + dx, 4)
        py = lax.rem(y + dy, 4)
        pc = 1 - core if other else core
        return ((px * 4 + py) * 2 + pc, lax.rem(z + dz, 8))

    peers = [at(other=True)]
    peers += [at(dx=d) for d in (1, 2, 3)] + [at(dy=d) for d in (1, 2, 3)]
    peers += [at(dz=d) for d in range(1, 8)]
    barrier = pltpu.get_barrier_semaphore()
    for peer in peers:
        pl.semaphore_signal(barrier, inc=1, device_id=peer, device_id_type=pl.DeviceIdType.MESH)

    copies = Copies(send_sems, recv_sems)
    iota = lax.broadcasted_iota(jnp.int32, (TILE, 1), 0)

    def load_tile(j):
        rows = pl.ds(pl.multiple_of(j * TILE, TILE), TILE)
        return pltpu.make_async_copy(c_hbm.at[rows], c_ref.at[rows], in_sems.at[j])

    a_copy = pltpu.make_async_copy(a_hbm, a_ref, in_sems.at[TILES])
    a_copy.start()
    for j in range(TILES):
        load_tile(j).start()
    a_copy.wait()
    al_hi[...], al_lo[...] = split(a_ref[...] * (SCALE * LOG2E))
    as_hi[...], as_lo[...] = split(a_ref[...] * SCALE)

    def logits_half(half):
        @pl.loop(0, TILES // 2)
        def _(step):
            for sub in range(2):
                j = step * 2 + sub
                rows = pl.ds(pl.multiple_of(j * TILE, TILE), TILE)
                if half == 0:
                    load_tile(j).wait()
                    block = c_ref[rows, :]
                    ch, cl = split(block)
                    c_hi[rows, :], c_lo[rows, :] = ch, cl
                    th, tl = split((block * SCALE).T)
                    ct_hi[j], ct_lo[j] = th, tl
                else:
                    ch, cl = c_hi[rows, :], c_lo[rows, :]
                left = jnp.concatenate([ch, cl, ch], axis=1)
                first = z * CANDS + j * TILE
                for i in (2 * half, 2 * half + 1):
                    lanes = slice(i * 256, (i + 1) * 256)
                    ah, al = al_hi[lanes, :], al_lo[lanes, :]
                    logits = dot_nt(left, jnp.concatenate([ah, ah, al], axis=1))
                    place = jnp.concatenate([pos_ref[2 * i], pos_ref[2 * i + 1]], axis=1)
                    hit = iota == place - first
                    top = jnp.max(logits, axis=0, keepdims=True)
                    stat[j, 2:3, lanes] = jnp.sum(jnp.where(hit, logits, 0.0), axis=0, keepdims=True)
                    prob = jnp.exp2(logits - top)
                    stat[j, 0:1, lanes] = top
                    stat[j, 1:2, lanes] = jnp.sum(prob, axis=0, keepdims=True)
                    p_ref[2 * i, rows, :] = prob[:, :128]
                    p_ref[2 * i + 1, rows, :] = prob[:, 128:]

    def send_stats(half):
        lanes = slice(half * 512, (half + 1) * 512)
        tops = [stat[j, 0:1, lanes] for j in range(TILES)]
        top = tops[0]
        for j in range(1, TILES):
            top = jnp.maximum(top, tops[j])
        total = jnp.zeros_like(top)
        chosen = jnp.zeros_like(top)
        for j in range(TILES):
            total += stat[j, 1:2, lanes] * jnp.exp2(tops[j] - top)
            chosen += stat[j, 2:3, lanes]
        for k in range(4):
            part = slice(k * 128, (k + 1) * 128)
            stat_rx[half, z, 0, k:k + 1, :] = top[:, part]
            stat_rx[half, z, 1, k:k + 1, :] = total[:, part]
            stat_rx[half, z, 2, k:k + 1, :] = chosen[:, part]
        mine = stat_rx.at[half, z]
        return [copies.start(mine, mine, at(dz=d)) for d in (4, 3, 5, 2, 6, 1, 7)]

    def take_stats(half, sent):
        for copy in sent:
            copy.wait_recv()
        top = stat_rx[half, 0, 0, 0:4, :]
        for k in range(1, 8):
            top = jnp.maximum(top, stat_rx[half, k, 0, 0:4, :])
        total = jnp.zeros_like(top)
        chosen = jnp.zeros_like(top)
        for k in range(8):
            total += stat_rx[half, k, 1, 0:4, :] * jnp.exp2(stat_rx[half, k, 0, 0:4, :] - top)
            chosen += stat_rx[half, k, 2, 0:4, :]
        lse = top + jnp.log2(total)
        loss_rx[0, core, half * 4:half * 4 + 4, :] = (lse - chosen) * LN2
        for k in range(4):
            chunk = half * 4 + k
            for j in range(TILES):
                back[chunk, j] = jnp.exp2(stat[j, 0:1, chunk * 128:(chunk + 1) * 128] - lse[k:k + 1, :])

    def cand_part(start, count, half):
        rows = pl.ds(pl.multiple_of(start, count), count)
        first = z * CANDS + start
        j = start // TILE
        highs, lows = [], []
        for k in range(4 * half, 4 * half + 4):
            weight = p_ref[k, rows, :] * back[k, j]
            hit = iota[:count] == pos_ref[k] - first
            wh, wl = split(jnp.where(hit, weight - 1.0, weight))
            w_hi[k, rows, :], w_lo[k, rows, :] = wh, wl
            highs.append(wh)
            lows.append(wl)
        wh, wl = jnp.concatenate(highs, axis=1), jnp.concatenate(lows, axis=1)
        ah = as_hi[half * 512:(half + 1) * 512, :]
        al = as_lo[half * 512:(half + 1) * 512, :]
        return dot(wh, ah) + dot(wl, ah) + dot(wh, al)

    def cand_first():
        @pl.loop(0, TILES // 2)
        def _(step):
            for sub in range(2):
                start = (step * 2 + sub) * TILE
                c_ref[pl.ds(pl.multiple_of(start, TILE), TILE), :] = cand_part(start, TILE, 0)

    def cand_blocks(spot, offsets):
        for n, (dx, dy) in enumerate(offsets):
            start = (lax.rem(x + dx, 4) * 4 + lax.rem(y + dy, 4)) * BLOCK
            rows = pl.ds(pl.multiple_of(start, BLOCK), BLOCK)
            part = c_ref[rows, :] + cand_part(start, BLOCK, 1)
            blocks[spot + n, 0] = part[:128, :]
            blocks[spot + n, 1] = part[128:, :]
        held = slice(spot, spot + len(offsets))
        return copies.start(blocks.at[held, 1 - core], pair_rx.at[held], at(other=True))

    def anchor_pair(pair):
        places = [lax.rem(z + d, 8) for d in pair]
        acc = None
        for j in range(TILES):
            rows = slice(j * TILE, (j + 1) * TILE)
            wh = jnp.concatenate([w_hi[p, rows, :] for p in places], axis=1)
            wl = jnp.concatenate([w_lo[p, rows, :] for p in places], axis=1)
            part = dot(ct_hi[j], wh) + dot(ct_lo[j], wh) + dot(ct_hi[j], wl)
            acc = part if acc is None else acc + part
        for n, d in enumerate(pair):
            grad[d] = acc[:, n * 128:(n + 1) * 128]

    logits_half(0)
    pl.semaphore_wait(barrier, len(peers))
    stats0 = send_stats(0)
    logits_half(1)
    stats1 = send_stats(1)
    take_stats(0, stats0)
    cand_first()
    take_stats(1, stats1)
    loss_copies = [copies.start(loss_rx.at[0, core], loss_rx.at[0, core], at(other=True))]

    pairs = [cand_blocks(3 * i, [(dx, dy) for dy in AWAY]) for i, dx in enumerate(AWAY)]
    pairs.append(cand_blocks(9, [(0, dy) for dy in AWAY]))
    pairs.append(cand_blocks(12, [(dx, 0) for dx in AWAY]))
    pairs.append(cand_blocks(15, [(0, 0)]))

    def paired(spot):
        return blocks[spot, core] + pair_rx[spot]

    def far_sum(i):
        pairs[i].wait_recv()
        for k in range(3):
            both = paired(3 * i + k)
            q0[i, k] = both[:, :128]
            q1[k, i] = both[:, 128:]

    top, low = slice(0, 64), slice(64, 128)

    def ring_far(ring, land, right, left):
        return [
            copies.start(ring.at[0, :, top], land.at[0], right),
            copies.start(ring.at[0, :, low], land.at[2], left),
        ]

    def ring_plain(ring, land, right, left):
        return [
            copies.start(ring.at[1, :, low], land.at[4], right),
            copies.start(ring.at[2, :, top], land.at[5], left),
        ]

    def ring_relay(ring, land, right, left, far):
        far[0].wait_recv()
        ring[1, :, top] = ring[1, :, top] + land[0]
        near = [copies.start(ring.at[1, :, top], land.at[1], right)]
        far[1].wait_recv()
        ring[2, :, low] = ring[2, :, low] + land[2]
        near.append(copies.start(ring.at[2, :, low], land.at[3], left))
        return near

    right_x, left_x, right_y, left_y = at(dx=1), at(dx=3), at(dy=1), at(dy=3)

    far_sum(0)
    x_far = ring_far(q0, rx0, right_x, left_x)
    for copy in loss_copies:
        copy.wait_recv()
    loss_rx[1, x] = loss_rx[0, 0] + loss_rx[0, 1]
    loss_copies = [copies.start(loss_rx.at[1, x], loss_rx.at[1, x], at(dx=d)) for d in AWAY]

    anchor_pair((4, 3))
    z_four = [
        copies.start(grad.at[4, 0:128], far_rx.at[0, 0:128], at(dz=2)),
        copies.start(grad.at[4, 128:256], far_rx.at[1, 128:256], at(dz=6)),
    ]
    z_three = [copies.start(grad.at[3], far_rx.at[2], at(dz=1))]
    far_sum(1)
    far_sum(2)
    y_far = ring_far(q1, ry1, right_y, left_y)
    x_near = ring_plain(q0, rx0, right_x, left_x)
    y_near = ring_plain(q1, ry1, right_y, left_y)

    anchor_pair((5, 2))
    z_three.append(copies.start(grad.at[5], far_rx.at[3], at(dz=7)))
    x_near += ring_relay(q0, rx0, right_x, left_x, x_far)
    for i in range(3):
        pairs[3 + min(i, 2)].wait_recv()
    for k in range(3):
        qa[k] = paired(9 + k)
        qb[k] = paired(12 + k)
    qo[...] = paired(15)
    for copy in loss_copies:
        copy.wait_recv()
    loss_rx[2, y] = (loss_rx[1, 0] + loss_rx[1, 1]) + (loss_rx[1, 2] + loss_rx[1, 3])
    loss_copies = [copies.start(loss_rx.at[2, y], loss_rx.at[2, y], at(dy=d)) for d in AWAY]

    anchor_pair((6, 1))
    z_last = [copies.start(grad.at[1], z_rx.at[0], at(dz=1))]
    y_near += ring_relay(q1, ry1, right_y, left_y, y_far)
    z_four[0].wait_recv()
    z_three[0].wait_recv()
    grad[2, 0:128] = grad[2, 0:128] + far_rx[0, 0:128] + far_rx[2, 0:128]
    grad[2, 128:256] = grad[2, 128:256] + far_rx[2, 128:256]
    z_last.append(copies.start(grad.at[2], z_rx.at[1], at(dz=2)))

    anchor_pair((7, 0))
    z_last.append(copies.start(grad.at[7], z_rx.at[2], at(dz=7)))
    z_four[1].wait_recv()
    z_three[1].wait_recv()
    grad[6, 0:128] = grad[6, 0:128] + far_rx[3, 0:128]
    grad[6, 128:256] = grad[6, 128:256] + far_rx[1, 128:256] + far_rx[3, 128:256]
    z_last.append(copies.start(grad.at[6], z_rx.at[3], at(dz=6)))

    last = []
    for copy in x_near:
        copy.wait_recv()
    for k, d in enumerate(AWAY):
        qa[k, top, 0:128] = qa[k, top, 0:128] + rx0[1, k] + rx0[5, k]
        qa[k, low, 0:128] = qa[k, low, 0:128] + rx0[3, k] + rx0[4, k]
        last.append(copies.start(qa.at[k], from_y.at[k], at(dy=d)))
    for copy in y_near:
        copy.wait_recv()
    for k, d in enumerate(AWAY):
        qb[k, top, 128:256] = qb[k, top, 128:256] + ry1[1, k] + ry1[5, k]
        qb[k, low, 128:256] = qb[k, low, 128:256] + ry1[3, k] + ry1[4, k]
        last.append(copies.start(qb.at[k], from_x.at[k], at(dx=d)))

    for copy in loss_copies:
        copy.wait_recv()
    losses = (loss_rx[2, 0] + loss_rx[2, 1]) + (loss_rx[2, 2] + loss_rx[2, 3])
    loss_ref[...] = jnp.sum(losses, keepdims=True) * (1.0 / (32 * ANCHORS))
    for copy in z_last:
        copy.wait_recv()
    agrad_ref[...] = (grad[0] + (z_rx[0] + z_rx[1]) + (z_rx[2] + z_rx[3])).T
    for copy in last:
        copy.wait_recv()
    cgrad_ref[...] = (
        qo[...] + (from_y[0] + from_y[1] + from_y[2]) + (from_x[0] + from_x[1] + from_x[2])
    )
    for copy in copies.made:
        copy.wait_send()


def body(anchors, candidates, positives):
    vmem = pl.BlockSpec(memory_space=pltpu.VMEM)
    hbm = pl.BlockSpec(memory_space=pl.ANY)
    sems = 64
    loss, anchor_grad, cand_grad = pl.pallas_call(
        kernel,
        out_shape=[
            jax.ShapeDtypeStruct((1, 1), F32),
            jax.ShapeDtypeStruct((128, WIDTH), F32),
            jax.ShapeDtypeStruct((128, WIDTH), F32),
        ],
        in_specs=[hbm, hbm, vmem],
        out_specs=[vmem] * 3,
        scratch_shapes=[
            pltpu.VMEM((ANCHORS, WIDTH), F32),
            pltpu.VMEM((CANDS, WIDTH), F32),
            pltpu.VMEM((CANDS, WIDTH), BF16),
            pltpu.VMEM((CANDS, WIDTH), BF16),
            pltpu.VMEM((TILES, WIDTH, TILE), BF16),
            pltpu.VMEM((TILES, WIDTH, TILE), BF16),
            pltpu.VMEM((ANCHORS, WIDTH), BF16),
            pltpu.VMEM((ANCHORS, WIDTH), BF16),
            pltpu.VMEM((ANCHORS, WIDTH), BF16),
            pltpu.VMEM((ANCHORS, WIDTH), BF16),
            pltpu.VMEM((8, CANDS, 128), F32),
            pltpu.VMEM((8, CANDS, 128), BF16),
            pltpu.VMEM((8, CANDS, 128), BF16),
            pltpu.VMEM((TILES, 8, ANCHORS), F32),
            pltpu.VMEM((8, TILES, 1, 128), F32),
            pltpu.VMEM((2, 8, 3, 8, 128), F32),
            pltpu.VMEM((3, 4, 8, 128), F32),
            pltpu.VMEM((16, 2, 128, WIDTH), F32),
            pltpu.VMEM((16, 128, WIDTH), F32),
            pltpu.VMEM((3, 3, 128, 128), F32),
            pltpu.VMEM((3, 3, 128, 128), F32),
            pltpu.VMEM((3, 128, WIDTH), F32),
            pltpu.VMEM((3, 128, WIDTH), F32),
            pltpu.VMEM((128, WIDTH), F32),
            pltpu.VMEM((6, 3, 64, 128), F32),
            pltpu.VMEM((6, 3, 64, 128), F32),
            pltpu.VMEM((3, 128, WIDTH), F32),
            pltpu.VMEM((3, 128, WIDTH), F32),
            pltpu.VMEM((8, WIDTH, 128), F32),
            pltpu.VMEM((4, WIDTH, 128), F32),
            pltpu.VMEM((4, WIDTH, 128), F32),
            pltpu.SemaphoreType.DMA((TILES + 1,)),
            pltpu.SemaphoreType.DMA((sems,)),
            pltpu.SemaphoreType.DMA((sems,)),
        ],
        compiler_params=pltpu.CompilerParams(
            collective_id=0, has_side_effects=True, vmem_limit_bytes=63 << 20
        ),
    )(anchors, candidates, positives.reshape(8, 1, 128))
    return (loss.reshape(()), anchor_grad, cand_grad[None])


def solution(mesh):
    in_specs = (P("anc", None), P("cand", None), P("anc"))
    out_specs = (P(), P(("anc", "cand"), None), P("cand", "anc", None))
    return jax.shard_map(body, mesh=mesh, in_specs=in_specs, out_specs=out_specs, check_vma=False)
```

```python
import math

import jax
import jax.numpy as jnp
from jax import lax
from jax.experimental import pallas as pl
from jax.experimental.pallas import tpu as pltpu
from jax.sharding import PartitionSpec as P

F32 = jnp.float32
BF16 = jnp.bfloat16
WIDTH = 256
ANCHORS = 1024
CANDS = 4096
TILE = 512
TILES = CANDS // TILE
LOG2E = math.log2(math.e)
LN2 = math.log(2.0)
SCALE = 0.25 / math.sqrt(WIDTH)
BLOCK = 256
PARTS = ((0, 6), (6, 8))
AWAY = (2, 1, 3)


def split(value):
    high = value.astype(BF16)
    return high, (value - high.astype(F32)).astype(BF16)


def dot(left, right):
    return jnp.dot(left, right, preferred_element_type=F32)


def dot_nt(left, right):
    return lax.dot_general(left, right, (((1,), (1,)), ((), ())), preferred_element_type=F32)


class Copies:
    def __init__(self, send_sems, recv_sems):
        self.send_sems, self.recv_sems = send_sems, recv_sems
        self.made = []

    def start(self, source, target, device):
        index = len(self.made)
        copy = pltpu.make_async_remote_copy(
            src_ref=source,
            dst_ref=target,
            send_sem=self.send_sems.at[index],
            recv_sem=self.recv_sems.at[index],
            device_id=device,
            device_id_type=pl.DeviceIdType.MESH,
        )
        copy.start()
        self.made.append(copy)
        return copy


def kernel(
    a_hbm, c_hbm, pos_ref, loss_ref, agrad_ref, cgrad_ref,
    a_ref, c_ref, c_hi, c_lo, ct_hi, ct_lo, al_hi, al_lo, as_hi, as_lo,
    p_ref, stat, back, stat_rx, loss_rx,
    blocks, pair_rx, q0, q1, qa, qb, rx0, ry1, from_y, from_x, grad, far_rx, z_rx,
    in_sems, send_sems, recv_sems,
):
    anc = lax.axis_index("anc")
    z = lax.axis_index("cand")
    x, y, core = anc // 8, lax.rem(anc // 2, 4), lax.rem(anc, 2)

    def at(dx=0, dy=0, other=False, dz=0):
        px = lax.rem(x + dx, 4)
        py = lax.rem(y + dy, 4)
        pc = 1 - core if other else core
        return ((px * 4 + py) * 2 + pc, lax.rem(z + dz, 8))

    peers = [at(other=True)]
    peers += [at(dx=d) for d in (1, 2, 3)] + [at(dy=d) for d in (1, 2, 3)]
    peers += [at(dz=d) for d in range(1, 8)]
    barrier = pltpu.get_barrier_semaphore()
    for peer in peers:
        pl.semaphore_signal(barrier, inc=1, device_id=peer, device_id_type=pl.DeviceIdType.MESH)

    copies = Copies(send_sems, recv_sems)
    iota = lax.broadcasted_iota(jnp.int32, (TILE, 1), 0)

    def load_tile(j):
        rows = pl.ds(pl.multiple_of(j * TILE, TILE), TILE)
        return pltpu.make_async_copy(c_hbm.at[rows], c_ref.at[rows], in_sems.at[j])

    a_copy = pltpu.make_async_copy(a_hbm, a_ref, in_sems.at[TILES])
    a_copy.start()
    for j in range(TILES):
        load_tile(j).start()
    a_copy.wait()
    al_hi[...], al_lo[...] = split(a_ref[...] * (SCALE * LOG2E))
    as_hi[...], as_lo[...] = split(a_ref[...] * SCALE)

    def logits_part(part):
        tiles = range(PARTS[part][0] // 2, PARTS[part][1] // 2)
        subs = 1 if part == 0 else 4

        @pl.loop(0, TILES // subs)
        def _(step):
            for sub in range(subs):
                j = step * subs + sub
                rows = pl.ds(pl.multiple_of(j * TILE, TILE), TILE)
                if part == 0:
                    load_tile(j).wait()
                    block = c_ref[rows, :]
                    ch, cl = split(block)
                    c_hi[rows, :], c_lo[rows, :] = ch, cl
                    th, tl = split((block * SCALE).T)
                    ct_hi[j], ct_lo[j] = th, tl
                else:
                    ch, cl = c_hi[rows, :], c_lo[rows, :]
                left = jnp.concatenate([ch, cl, ch], axis=1)
                first = z * CANDS + j * TILE
                for i in tiles:
                    lanes = slice(i * 256, (i + 1) * 256)
                    ah, al = al_hi[lanes, :], al_lo[lanes, :]
                    logits = dot_nt(left, jnp.concatenate([ah, ah, al], axis=1))
                    place = jnp.concatenate([pos_ref[2 * i], pos_ref[2 * i + 1]], axis=1)
                    hit = iota == place - first
                    top = jnp.max(logits, axis=0, keepdims=True)
                    stat[j, 2:3, lanes] = jnp.sum(jnp.where(hit, logits, 0.0), axis=0, keepdims=True)
                    prob = jnp.exp2(logits - top)
                    stat[j, 0:1, lanes] = top
                    stat[j, 1:2, lanes] = jnp.sum(prob, axis=0, keepdims=True)
                    p_ref[2 * i, rows, :] = prob[:, :128]
                    p_ref[2 * i + 1, rows, :] = prob[:, 128:]

    def send_stats(part):
        lo, hi = PARTS[part]
        lanes = slice(lo * 128, hi * 128)
        tops = [stat[j, 0:1, lanes] for j in range(TILES)]
        top = tops[0]
        for j in range(1, TILES):
            top = jnp.maximum(top, tops[j])
        total = jnp.zeros_like(top)
        chosen = jnp.zeros_like(top)
        for j in range(TILES):
            total += stat[j, 1:2, lanes] * jnp.exp2(tops[j] - top)
            chosen += stat[j, 2:3, lanes]
        for k in range(hi - lo):
            piece = slice(k * 128, (k + 1) * 128)
            stat_rx[part, z, 0, k:k + 1, :] = top[:, piece]
            stat_rx[part, z, 1, k:k + 1, :] = total[:, piece]
            stat_rx[part, z, 2, k:k + 1, :] = chosen[:, piece]
        mine = stat_rx.at[part, z]
        return [copies.start(mine, mine, at(dz=d)) for d in (4, 3, 5, 2, 6, 1, 7)]

    def take_stats(part, sent):
        for copy in sent:
            copy.wait_recv()
        lo, hi = PARTS[part]
        used = slice(0, hi - lo)
        top = stat_rx[part, 0, 0, used, :]
        for k in range(1, 8):
            top = jnp.maximum(top, stat_rx[part, k, 0, used, :])
        total = jnp.zeros_like(top)
        chosen = jnp.zeros_like(top)
        for k in range(8):
            total += stat_rx[part, k, 1, used, :] * jnp.exp2(stat_rx[part, k, 0, used, :] - top)
            chosen += stat_rx[part, k, 2, used, :]
        lse = top + jnp.log2(total)
        loss_rx[0, core, lo:hi, :] = (lse - chosen) * LN2
        for k in range(lo, hi):
            for j in range(TILES):
                back[k, j] = jnp.exp2(stat[j, 0:1, k * 128:(k + 1) * 128] - lse[k - lo:k - lo + 1, :])

    def weights(k, rows, count, first, j):
        weight = p_ref[k, rows, :] * back[k, j]
        hit = iota[:count] == pos_ref[k] - first
        return split(jnp.where(hit, weight - 1.0, weight))

    def cand_blocks(spot, offsets, lo, hi):
        for n, (dx, dy) in enumerate(offsets):
            start = (lax.rem(x + dx, 4) * 4 + lax.rem(y + dy, 4)) * BLOCK
            rows = pl.ds(pl.multiple_of(start, BLOCK), BLOCK)
            both = [weights(k, rows, BLOCK, z * CANDS + start, start // TILE) for k in range(lo, hi)]
            wh = jnp.concatenate([w[0] for w in both], axis=1)
            wl = jnp.concatenate([w[1] for w in both], axis=1)
            ah, al = as_hi[lo * 128:hi * 128, :], as_lo[lo * 128:hi * 128, :]
            part = dot(wh, ah) + dot(wl, ah) + dot(wh, al)
            for c in range(2):
                mine = part[c * 128:(c + 1) * 128, :]
                blocks[spot + n, c] = mine if lo == 0 else blocks[spot + n, c] + mine

    def cand_send(spot, count):
        held = slice(spot, spot + count)
        return copies.start(blocks.at[held, 1 - core], pair_rx.at[held], at(other=True))

    def anchor_pair(pair):
        places = [lax.rem(z + d, 8) for d in pair]
        acc = None
        for j in range(TILES):
            rows = slice(j * TILE, (j + 1) * TILE)
            both = [weights(p, rows, TILE, z * CANDS + j * TILE, j) for p in places]
            wh = jnp.concatenate([w[0] for w in both], axis=1)
            wl = jnp.concatenate([w[1] for w in both], axis=1)
            part = dot(ct_hi[j], wh) + dot(ct_lo[j], wh) + dot(ct_hi[j], wl)
            acc = part if acc is None else acc + part
        for n, d in enumerate(pair):
            grad[d] = acc[:, n * 128:(n + 1) * 128]

    def paired(spot):
        return blocks[spot, core] + pair_rx[spot]

    def far_send(i):
        pairs[i].wait_recv()
        for k in range(3):
            both = paired(3 * i + k)
            q0[i, k] = both[:, :128]
            q1[i, k] = both[:, 128:]
        sent = [copies.start(q0.at[i], rx0.at[i], at(dx=AWAY[i]))]
        return sent + [copies.start(q1.at[i, k], ry1.at[i, k], at(dy=AWAY[k])) for k in range(3)]

    low, high = slice(0, 128), slice(128, 256)
    logits_part(0)
    pl.semaphore_wait(barrier, len(peers))
    stats0 = send_stats(0)
    logits_part(1)
    stats1 = send_stats(1)
    take_stats(0, stats0)
    spots = [(3 * i, [(dx, dy) for dy in AWAY]) for i, dx in enumerate(AWAY)]
    spots += [(9, [(0, dy) for dy in AWAY]), (12, [(dx, 0) for dx in AWAY])]
    for spot, offsets in spots:
        cand_blocks(spot, offsets, 0, 6)
    take_stats(1, stats1)
    loss_copies = [copies.start(loss_rx.at[0, core], loss_rx.at[0, core], at(other=True))]

    anchor_pair((4, 3))
    to_two = [
        copies.start(grad.at[4, low], far_rx.at[0, low], at(dz=2)),
        copies.start(grad.at[3], far_rx.at[2], at(dz=1)),
    ]
    to_six = [copies.start(grad.at[4, high], far_rx.at[1, high], at(dz=6))]
    pairs = []
    for spot, offsets in spots[:3]:
        cand_blocks(spot, offsets, 6, 8)
        pairs.append(cand_send(spot, 3))
    far = far_send(0) + far_send(1)

    anchor_pair((5, 2))
    to_six.append(copies.start(grad.at[5], far_rx.at[3], at(dz=7)))
    far += far_send(2)
    for copy in loss_copies:
        copy.wait_recv()
    loss_rx[1, x] = loss_rx[0, 0] + loss_rx[0, 1]
    loss_copies = [copies.start(loss_rx.at[1, x], loss_rx.at[1, x], at(dx=d)) for d in AWAY]
    for spot, offsets in spots[3:]:
        cand_blocks(spot, offsets, 6, 8)
        pairs.append(cand_send(spot, 3))

    anchor_pair((6, 1))
    z_last = [copies.start(grad.at[1], z_rx.at[0], at(dz=1))]
    last = []
    pairs[3].wait_recv()
    pairs[4].wait_recv()
    for k, d in enumerate(AWAY):
        mine = paired(9 + k)
        qa[k, 0], qa[k, 1] = mine[:, :128], mine[:, 128:]
        last.append(copies.start(qa.at[k, 1], from_y.at[k, 1], at(dy=d)))
        mine = paired(12 + k)
        qb[k, 0], qb[k, 1] = mine[:, :128], mine[:, 128:]
        last.append(copies.start(qb.at[k, 0], from_x.at[k, 0], at(dx=d)))
    for copy in loss_copies:
        copy.wait_recv()
    loss_rx[2, y] = (loss_rx[1, 0] + loss_rx[1, 1]) + (loss_rx[1, 2] + loss_rx[1, 3])
    loss_copies = [copies.start(loss_rx.at[2, y], loss_rx.at[2, y], at(dy=d)) for d in AWAY]

    anchor_pair((7, 0))
    z_last.append(copies.start(grad.at[7], z_rx.at[1], at(dz=7)))
    for copy in to_two:
        copy.wait_recv()
    grad[2, low] = grad[2, low] + far_rx[0, low] + far_rx[2, low]
    grad[2, high] = grad[2, high] + far_rx[2, high]
    z_last.append(copies.start(grad.at[2], z_rx.at[2], at(dz=2)))
    for copy in to_six:
        copy.wait_recv()
    grad[6, low] = grad[6, low] + far_rx[3, low]
    grad[6, high] = grad[6, high] + far_rx[1, high] + far_rx[3, high]
    z_last.append(copies.start(grad.at[6], z_rx.at[3], at(dz=6)))

    cand_blocks(15, [(0, 0)], 0, 8)
    pairs.append(cand_send(15, 1))
    for copy in far:
        copy.wait_recv()
    for k, d in enumerate(AWAY):
        qa[k, 0] = qa[k, 0] + (rx0[0, k] + rx0[1, k] + rx0[2, k])
        last.append(copies.start(qa.at[k, 0], from_y.at[k, 0], at(dy=d)))
        qb[k, 1] = qb[k, 1] + (ry1[k, 0] + ry1[k, 1] + ry1[k, 2])
        last.append(copies.start(qb.at[k, 1], from_x.at[k, 1], at(dx=d)))

    for copy in loss_copies:
        copy.wait_recv()
    losses = (loss_rx[2, 0] + loss_rx[2, 1]) + (loss_rx[2, 2] + loss_rx[2, 3])
    loss_ref[...] = jnp.sum(losses, keepdims=True) * (1.0 / (32 * ANCHORS))
    for copy in z_last:
        copy.wait_recv()
    agrad_ref[...] = (grad[0] + (z_rx[0] + z_rx[1]) + (z_rx[2] + z_rx[3])).T
    pairs[5].wait_recv()
    for copy in last:
        copy.wait_recv()
    own = paired(15)
    for h in range(2):
        lanes = slice(h * 128, (h + 1) * 128)
        cgrad_ref[:, lanes] = own[:, lanes] + (
            (from_y[0, h] + from_y[1, h] + from_y[2, h]) + (from_x[0, h] + from_x[1, h] + from_x[2, h])
        )
    for copy in copies.made:
        copy.wait_send()


def body(anchors, candidates, positives):
    vmem = pl.BlockSpec(memory_space=pltpu.VMEM)
    hbm = pl.BlockSpec(memory_space=pl.ANY)
    sems = 64
    grads = [jax.ShapeDtypeStruct((128, WIDTH), F32)] * 2
    loss, anchor_grad, cand_grad = pl.pallas_call(
        kernel,
        out_shape=[jax.ShapeDtypeStruct((1, 1), F32)] + grads,
        in_specs=[hbm, hbm, vmem],
        out_specs=[vmem] * 3,
        scratch_shapes=[
            pltpu.VMEM((ANCHORS, WIDTH), F32),
            pltpu.VMEM((CANDS, WIDTH), F32),
            pltpu.VMEM((CANDS, WIDTH), BF16),
            pltpu.VMEM((CANDS, WIDTH), BF16),
            pltpu.VMEM((TILES, WIDTH, TILE), BF16),
            pltpu.VMEM((TILES, WIDTH, TILE), BF16),
            pltpu.VMEM((ANCHORS, WIDTH), BF16),
            pltpu.VMEM((ANCHORS, WIDTH), BF16),
            pltpu.VMEM((ANCHORS, WIDTH), BF16),
            pltpu.VMEM((ANCHORS, WIDTH), BF16),
            pltpu.VMEM((8, CANDS, 128), F32),
            pltpu.VMEM((TILES, 8, ANCHORS), F32),
            pltpu.VMEM((8, TILES, 1, 128), F32),
            pltpu.VMEM((2, 8, 3, 8, 128), F32),
            pltpu.VMEM((3, 4, 8, 128), F32),
            pltpu.VMEM((16, 2, 128, WIDTH), F32),
            pltpu.VMEM((16, 128, WIDTH), F32),
            pltpu.VMEM((3, 3, 128, 128), F32),
            pltpu.VMEM((3, 3, 128, 128), F32),
            pltpu.VMEM((3, 2, 128, 128), F32),
            pltpu.VMEM((3, 2, 128, 128), F32),
            pltpu.VMEM((3, 3, 128, 128), F32),
            pltpu.VMEM((3, 3, 128, 128), F32),
            pltpu.VMEM((3, 2, 128, 128), F32),
            pltpu.VMEM((3, 2, 128, 128), F32),
            pltpu.VMEM((8, WIDTH, 128), F32),
            pltpu.VMEM((4, WIDTH, 128), F32),
            pltpu.VMEM((4, WIDTH, 128), F32),
            pltpu.SemaphoreType.DMA((TILES + 1,)),
            pltpu.SemaphoreType.DMA((sems,)),
            pltpu.SemaphoreType.DMA((sems,)),
        ],
        compiler_params=pltpu.CompilerParams(
            collective_id=0, has_side_effects=True, vmem_limit_bytes=63 << 20
        ),
    )(anchors, candidates, positives.reshape(8, 1, 128))
    return (loss.reshape(()), anchor_grad, cand_grad[None])


def solution(mesh):
    in_specs = (P("anc", None), P("cand", None), P("anc"))
    out_specs = (P(), P(("anc", "cand"), None), P("cand", "anc", None))
    return jax.shard_map(body, mesh=mesh, in_specs=in_specs, out_specs=out_specs, check_vma=False)
```

```python
import math

import jax
import jax.numpy as jnp
from jax import lax
from jax.experimental import pallas as pl
from jax.experimental.pallas import tpu as pltpu
from jax.sharding import PartitionSpec as P

F32 = jnp.float32
BF16 = jnp.bfloat16
WIDTH = 256
ANCHORS = 1024
CANDS = 4096
TILE = 512
TILES = CANDS // TILE
LOG2E = math.log2(math.e)
LN2 = math.log(2.0)
SCALE = 0.25 / math.sqrt(WIDTH)
BLOCK = 256
CHUNKS = (0, 2, 4, 6, 1, 3, 5, 7)
AWAY = (2, 1, 3)


def split(value):
    high = value.astype(BF16)
    return high, (value - high.astype(F32)).astype(BF16)


def dot(left, right):
    return jnp.dot(left, right, preferred_element_type=F32)


def dot_nt(left, right):
    return lax.dot_general(left, right, (((1,), (1,)), ((), ())), preferred_element_type=F32)


class Copies:
    def __init__(self, send_sems, recv_sems):
        self.send_sems, self.recv_sems = send_sems, recv_sems
        self.made = []

    def start(self, source, target, device):
        index = len(self.made)
        copy = pltpu.make_async_remote_copy(
            src_ref=source,
            dst_ref=target,
            send_sem=self.send_sems.at[index],
            recv_sem=self.recv_sems.at[index],
            device_id=device,
            device_id_type=pl.DeviceIdType.MESH,
        )
        copy.start()
        self.made.append(copy)
        return copy


def kernel(
    a_hbm, c_hbm, pos_ref, loss_ref, agrad_ref, cgrad_ref,
    a_ref, c_ref, c_hi, c_lo, ct_hi, ct_lo, al_hi, al_lo, as_hi, as_lo,
    p_ref, stat, back, stat_rx, loss_rx,
    blocks, pair_rx, q0, q1, qa, qb, rx0, ry1, from_y, from_x, grad, z_rx, z_send, z_recv,
    in_sems, send_sems, recv_sems,
):
    anc = lax.axis_index("anc")
    z = lax.axis_index("cand")
    x, y, core = anc // 8, lax.rem(anc // 2, 4), lax.rem(anc, 2)

    def at(dx=0, dy=0, other=False, dz=0):
        px = lax.rem(x + dx, 4)
        py = lax.rem(y + dy, 4)
        pc = 1 - core if other else core
        return ((px * 4 + py) * 2 + pc, lax.rem(z + dz, 8))

    peers = [at(other=True)]
    peers += [at(dx=d) for d in (1, 2, 3)] + [at(dy=d) for d in (1, 2, 3)]
    peers += [at(dz=d) for d in range(1, 8)]
    barrier = pltpu.get_barrier_semaphore()
    for peer in peers:
        pl.semaphore_signal(barrier, inc=1, device_id=peer, device_id_type=pl.DeviceIdType.MESH)

    copies = Copies(send_sems, recv_sems)
    iota = lax.broadcasted_iota(jnp.int32, (TILE, 1), 0)

    def load_tile(j):
        rows = pl.ds(pl.multiple_of(j * TILE, TILE), TILE)
        return pltpu.make_async_copy(c_hbm.at[rows], c_ref.at[rows], in_sems.at[j])

    a_copies = []
    for q, chunk in enumerate(CHUNKS):
        a_copies.append(pltpu.make_async_copy(
            a_hbm.at[pl.ds(chunk * 128, 128)], a_ref.at[pl.ds(q * 128, 128)], in_sems.at[TILES + q]
        ))
        a_copies[-1].start()
    for j in range(TILES):
        load_tile(j).start()
    for copy in a_copies:
        copy.wait()
    al_hi[...], al_lo[...] = split(a_ref[...] * (SCALE * LOG2E))
    as_hi[...], as_lo[...] = split(a_ref[...] * SCALE)

    def logits_part(part):
        tiles = (2 * part, 2 * part + 1)
        subs = 2

        @pl.loop(0, TILES // subs)
        def _(step):
            for sub in range(subs):
                j = step * subs + sub
                rows = pl.ds(pl.multiple_of(j * TILE, TILE), TILE)
                if part == 0:
                    load_tile(j).wait()
                    block = c_ref[rows, :]
                    ch, cl = split(block)
                    c_hi[rows, :], c_lo[rows, :] = ch, cl
                    th, tl = split((block * SCALE).T)
                    ct_hi[j], ct_lo[j] = th, tl
                else:
                    ch, cl = c_hi[rows, :], c_lo[rows, :]
                left = jnp.concatenate([ch, cl, ch], axis=1)
                first = z * CANDS + j * TILE
                for i in tiles:
                    lanes = slice(i * 256, (i + 1) * 256)
                    ah, al = al_hi[lanes, :], al_lo[lanes, :]
                    logits = dot_nt(left, jnp.concatenate([ah, ah, al], axis=1))
                    place = jnp.concatenate([pos_ref[CHUNKS[2 * i]], pos_ref[CHUNKS[2 * i + 1]]], axis=1)
                    hit = iota == place - first
                    top = jnp.max(logits, axis=0, keepdims=True)
                    stat[j, 2:3, lanes] = jnp.sum(jnp.where(hit, logits, 0.0), axis=0, keepdims=True)
                    prob = jnp.exp2(logits - top)
                    stat[j, 0:1, lanes] = top
                    stat[j, 1:2, lanes] = jnp.sum(prob, axis=0, keepdims=True)
                    p_ref[2 * i, rows, :] = prob[:, :128]
                    p_ref[2 * i + 1, rows, :] = prob[:, 128:]

    def send_stats(part):
        lo, hi = 4 * part, 4 * part + 4
        lanes = slice(lo * 128, hi * 128)
        tops = [stat[j, 0:1, lanes] for j in range(TILES)]
        top = tops[0]
        for j in range(1, TILES):
            top = jnp.maximum(top, tops[j])
        total = jnp.zeros_like(top)
        chosen = jnp.zeros_like(top)
        for j in range(TILES):
            total += stat[j, 1:2, lanes] * jnp.exp2(tops[j] - top)
            chosen += stat[j, 2:3, lanes]
        for k in range(hi - lo):
            piece = slice(k * 128, (k + 1) * 128)
            stat_rx[part, z, 0, k:k + 1, :] = top[:, piece]
            stat_rx[part, z, 1, k:k + 1, :] = total[:, piece]
            stat_rx[part, z, 2, k:k + 1, :] = chosen[:, piece]
        mine = stat_rx.at[part, z]
        return [copies.start(mine, mine, at(dz=d)) for d in (4, 3, 5, 2, 6, 1, 7)]

    def take_stats(part, sent):
        for copy in sent:
            copy.wait_recv()
        lo, hi = 4 * part, 4 * part + 4
        used = slice(0, hi - lo)
        top = stat_rx[part, 0, 0, used, :]
        for k in range(1, 8):
            top = jnp.maximum(top, stat_rx[part, k, 0, used, :])
        total = jnp.zeros_like(top)
        chosen = jnp.zeros_like(top)
        for k in range(8):
            total += stat_rx[part, k, 1, used, :] * jnp.exp2(stat_rx[part, k, 0, used, :] - top)
            chosen += stat_rx[part, k, 2, used, :]
        lse = top + jnp.log2(total)
        loss_rx[0, core, lo:hi, :] = (lse - chosen) * LN2
        for k in range(lo, hi):
            for j in range(TILES):
                back[k, j] = jnp.exp2(stat[j, 0:1, k * 128:(k + 1) * 128] - lse[k - lo:k - lo + 1, :])

    def weights(q, chunk, rows, count, first, j):
        weight = p_ref[q, rows, :] * back[q, j]
        hit = iota[:count] == pos_ref[chunk] - first
        return split(jnp.where(hit, weight - 1.0, weight))

    def cand_blocks(spot, offsets):
        for n, (dx, dy) in enumerate(offsets):
            start = (lax.rem(x + dx, 4) * 4 + lax.rem(y + dy, 4)) * BLOCK
            rows = pl.ds(pl.multiple_of(start, BLOCK), BLOCK)
            first = z * CANDS + start
            both = [weights(q, CHUNKS[q], rows, BLOCK, first, start // TILE) for q in range(8)]
            wh = jnp.concatenate([w[0] for w in both], axis=1)
            wl = jnp.concatenate([w[1] for w in both], axis=1)
            part = dot(wh, as_hi[...]) + dot(wl, as_hi[...]) + dot(wh, as_lo[...])
            blocks[spot + n, 0] = part[:128, :]
            blocks[spot + n, 1] = part[128:, :]
        return cand_send(spot, len(offsets))

    def cand_send(spot, count):
        held = slice(spot, spot + count)
        return copies.start(blocks.at[held, 1 - core], pair_rx.at[held], at(other=True))

    odd = lax.rem(z, 2)

    def offset(part, k):
        return (odd if part == 0 else 1 - odd) + 2 * k

    def anchor_pair(part, pair):
        places = [lax.rem(z + offset(part, k), 8) for k in pair]
        acc = None
        for j in range(TILES):
            rows = slice(j * TILE, (j + 1) * TILE)
            both = [
                weights(4 * part + p // 2, p, rows, TILE, z * CANDS + j * TILE, j) for p in places
            ]
            wh = jnp.concatenate([w[0] for w in both], axis=1)
            wl = jnp.concatenate([w[1] for w in both], axis=1)
            product = dot(ct_hi[j], wh) + dot(ct_lo[j], wh) + dot(ct_hi[j], wl)
            acc = product if acc is None else acc + product
        for n, k in enumerate(pair):
            grad[4 * part + k] = acc[:, n * 128:(n + 1) * 128]
            copy = grad_copy(part, k)
            if k == 0:
                pl.when(odd == 1 - part)(copy.start)
            else:
                copy.start()

    def grad_copy(part, k):
        away = offset(part, k)
        return pltpu.make_async_remote_copy(
            src_ref=grad.at[4 * part + k],
            dst_ref=z_rx.at[away],
            send_sem=z_send.at[4 * part + k if k else 0],
            recv_sem=z_recv.at[away],
            device_id=(anc, lax.rem(z + away, 8)),
            device_id_type=pl.DeviceIdType.MESH,
        )

    def paired(spot):
        return blocks[spot, core] + pair_rx[spot]

    def far_send(i):
        pairs[i].wait_recv()
        for k in range(3):
            both = paired(3 * i + k)
            q0[i, k] = both[:, :128]
            q1[i, k] = both[:, 128:]
        sent = [copies.start(q0.at[i], rx0.at[i], at(dx=AWAY[i]))]
        return sent + [copies.start(q1.at[i, k], ry1.at[i, k], at(dy=AWAY[k])) for k in range(3)]

    logits_part(0)
    pl.semaphore_wait(barrier, len(peers))
    stats0 = send_stats(0)
    logits_part(1)
    stats1 = send_stats(1)
    take_stats(0, stats0)
    anchor_pair(0, (2, 1))
    anchor_pair(0, (3, 0))
    take_stats(1, stats1)
    loss_copies = [copies.start(loss_rx.at[0, core], loss_rx.at[0, core], at(other=True))]
    pairs = [cand_blocks(3 * i, [(dx, dy) for dy in AWAY]) for i, dx in enumerate(AWAY)]
    far = far_send(0) + far_send(1)

    anchor_pair(1, (2, 1))
    far += far_send(2)
    for copy in loss_copies:
        copy.wait_recv()
    loss_rx[1, x] = loss_rx[0, 0] + loss_rx[0, 1]
    loss_copies = [copies.start(loss_rx.at[1, x], loss_rx.at[1, x], at(dx=d)) for d in AWAY]
    pairs.append(cand_blocks(9, [(0, dy) for dy in AWAY]))
    pairs.append(cand_blocks(12, [(dx, 0) for dx in AWAY]))

    anchor_pair(1, (3, 0))
    last = []
    pairs[3].wait_recv()
    pairs[4].wait_recv()
    for k, d in enumerate(AWAY):
        mine = paired(9 + k)
        qa[k, 0], qa[k, 1] = mine[:, :128], mine[:, 128:]
        last.append(copies.start(qa.at[k, 1], from_y.at[k, 1], at(dy=d)))
        mine = paired(12 + k)
        qb[k, 0], qb[k, 1] = mine[:, :128], mine[:, 128:]
        last.append(copies.start(qb.at[k, 0], from_x.at[k, 0], at(dx=d)))
    for copy in loss_copies:
        copy.wait_recv()
    loss_rx[2, y] = (loss_rx[1, 0] + loss_rx[1, 1]) + (loss_rx[1, 2] + loss_rx[1, 3])
    loss_copies = [copies.start(loss_rx.at[2, y], loss_rx.at[2, y], at(dy=d)) for d in AWAY]

    pairs.append(cand_blocks(15, [(0, 0)]))
    for copy in far:
        copy.wait_recv()
    for k, d in enumerate(AWAY):
        qa[k, 0] = qa[k, 0] + (rx0[0, k] + rx0[1, k] + rx0[2, k])
        last.append(copies.start(qa.at[k, 0], from_y.at[k, 0], at(dy=d)))
        qb[k, 1] = qb[k, 1] + (ry1[k, 0] + ry1[k, 1] + ry1[k, 2])
        last.append(copies.start(qb.at[k, 1], from_x.at[k, 1], at(dx=d)))

    for copy in loss_copies:
        copy.wait_recv()
    losses = (loss_rx[2, 0] + loss_rx[2, 1]) + (loss_rx[2, 2] + loss_rx[2, 3])
    loss_ref[...] = jnp.sum(losses, keepdims=True) * (1.0 / (32 * ANCHORS))
    for away in range(1, 8):
        pltpu.make_async_remote_copy(
            src_ref=grad.at[away],
            dst_ref=z_rx.at[away],
            send_sem=z_send.at[away],
            recv_sem=z_recv.at[away],
            device_id=at(dz=1),
            device_id_type=pl.DeviceIdType.MESH,
        ).wait_recv()
    near = (z_rx[1] + z_rx[2]) + (z_rx[6] + z_rx[7])
    agrad_ref[...] = (grad[4 * odd] + near + (z_rx[3] + z_rx[4]) + z_rx[5]).T
    pairs[5].wait_recv()
    for copy in last:
        copy.wait_recv()
    own = paired(15)
    for h in range(2):
        lanes = slice(h * 128, (h + 1) * 128)
        cgrad_ref[:, lanes] = own[:, lanes] + (
            (from_y[0, h] + from_y[1, h] + from_y[2, h]) + (from_x[0, h] + from_x[1, h] + from_x[2, h])
        )
    for copy in copies.made:
        copy.wait_send()
    for part, k in ((0, 0), (0, 1), (0, 2), (0, 3), (1, 1), (1, 2), (1, 3)):
        grad_copy(part, k).wait_send()


def body(anchors, candidates, positives):
    vmem = pl.BlockSpec(memory_space=pltpu.VMEM)
    hbm = pl.BlockSpec(memory_space=pl.ANY)
    sems = 64
    grads = [jax.ShapeDtypeStruct((128, WIDTH), F32)] * 2
    loss, anchor_grad, cand_grad = pl.pallas_call(
        kernel,
        out_shape=[jax.ShapeDtypeStruct((1, 1), F32)] + grads,
        in_specs=[hbm, hbm, vmem],
        out_specs=[vmem] * 3,
        scratch_shapes=[
            pltpu.VMEM((ANCHORS, WIDTH), F32),
            pltpu.VMEM((CANDS, WIDTH), F32),
            pltpu.VMEM((CANDS, WIDTH), BF16),
            pltpu.VMEM((CANDS, WIDTH), BF16),
            pltpu.VMEM((TILES, WIDTH, TILE), BF16),
            pltpu.VMEM((TILES, WIDTH, TILE), BF16),
            pltpu.VMEM((ANCHORS, WIDTH), BF16),
            pltpu.VMEM((ANCHORS, WIDTH), BF16),
            pltpu.VMEM((ANCHORS, WIDTH), BF16),
            pltpu.VMEM((ANCHORS, WIDTH), BF16),
            pltpu.VMEM((8, CANDS, 128), F32),
            pltpu.VMEM((TILES, 8, ANCHORS), F32),
            pltpu.VMEM((8, TILES, 1, 128), F32),
            pltpu.VMEM((2, 8, 3, 8, 128), F32),
            pltpu.VMEM((3, 4, 8, 128), F32),
            pltpu.VMEM((16, 2, 128, WIDTH), F32),
            pltpu.VMEM((16, 128, WIDTH), F32),
            pltpu.VMEM((3, 3, 128, 128), F32),
            pltpu.VMEM((3, 3, 128, 128), F32),
            pltpu.VMEM((3, 2, 128, 128), F32),
            pltpu.VMEM((3, 2, 128, 128), F32),
            pltpu.VMEM((3, 3, 128, 128), F32),
            pltpu.VMEM((3, 3, 128, 128), F32),
            pltpu.VMEM((3, 2, 128, 128), F32),
            pltpu.VMEM((3, 2, 128, 128), F32),
            pltpu.VMEM((8, WIDTH, 128), F32),
            pltpu.VMEM((8, WIDTH, 128), F32),
            pltpu.SemaphoreType.DMA((8,)),
            pltpu.SemaphoreType.DMA((8,)),
            pltpu.SemaphoreType.DMA((TILES + 8,)),
            pltpu.SemaphoreType.DMA((sems,)),
            pltpu.SemaphoreType.DMA((sems,)),
        ],
        compiler_params=pltpu.CompilerParams(
            collective_id=0, has_side_effects=True, vmem_limit_bytes=63 << 20
        ),
    )(anchors, candidates, positives.reshape(8, 1, 128))
    return (loss.reshape(()), anchor_grad, cand_grad[None])


def solution(mesh):
    in_specs = (P("anc", None), P("cand", None), P("anc"))
    out_specs = (P(), P(("anc", "cand"), None), P("cand", "anc", None))
    return jax.shard_map(body, mesh=mesh, in_specs=in_specs, out_specs=out_specs, check_vma=False)
```

```python
import math

import jax
import jax.numpy as jnp
from jax import lax
from jax.experimental import pallas as pl
from jax.experimental.pallas import tpu as pltpu
from jax.sharding import PartitionSpec as P

F32 = jnp.float32
BF16 = jnp.bfloat16
WIDTH = 256
ANCHORS = 1024
CANDS = 4096
TILE = 512
TILES = CANDS // TILE
LOG2E = math.log2(math.e)
LN2 = math.log(2.0)
SCALE = 0.25 / math.sqrt(WIDTH)
BLOCK = 256
CHUNKS = (0, 2, 4, 6, 1, 3, 5, 7)
AWAY = (2, 1, 3)


def split(value):
    high = value.astype(BF16)
    return high, (value - high.astype(F32)).astype(BF16)


def dot(left, right):
    return jnp.dot(left, right, preferred_element_type=F32)


def dot_nt(left, right):
    return lax.dot_general(left, right, (((1,), (1,)), ((), ())), preferred_element_type=F32)


class Copies:
    def __init__(self, send_sems, recv_sems):
        self.send_sems, self.recv_sems = send_sems, recv_sems
        self.made = []

    def start(self, source, target, device):
        index = len(self.made)
        copy = pltpu.make_async_remote_copy(
            src_ref=source,
            dst_ref=target,
            send_sem=self.send_sems.at[index],
            recv_sem=self.recv_sems.at[index],
            device_id=device,
            device_id_type=pl.DeviceIdType.MESH,
        )
        copy.start()
        self.made.append(copy)
        return copy


def kernel(
    a_hbm, c_hbm, pos_ref, loss_ref, agrad_ref, cgrad_ref,
    a_ref, c_ref, c_hi, c_lo, ct_hi, ct_lo, al_hi, al_lo, as_hi, as_lo,
    p_ref, stat, back, stat_rx, loss_rx,
    blocks, pair_rx, q0, q1, qa, qb, rx0, ry1, from_y, from_x, grad, z_rx, z_send, z_recv,
    in_sems, send_sems, recv_sems,
):
    anc = lax.axis_index("anc")
    z = lax.axis_index("cand")
    x, y, core = anc // 8, lax.rem(anc // 2, 4), lax.rem(anc, 2)

    def at(dx=0, dy=0, other=False, dz=0):
        px = lax.rem(x + dx, 4)
        py = lax.rem(y + dy, 4)
        pc = 1 - core if other else core
        return ((px * 4 + py) * 2 + pc, lax.rem(z + dz, 8))

    peers = [at(other=True)]
    peers += [at(dx=d) for d in (1, 2, 3)] + [at(dy=d) for d in (1, 2, 3)]
    peers += [at(dz=d) for d in range(1, 8)]
    copies = Copies(send_sems, recv_sems)
    iota = lax.broadcasted_iota(jnp.int32, (TILE, 1), 0)

    def load_tile(j):
        rows = pl.ds(pl.multiple_of(j * TILE, TILE), TILE)
        return pltpu.make_async_copy(c_hbm.at[rows], c_ref.at[rows], in_sems.at[j])

    a_copies = []
    for q, chunk in enumerate(CHUNKS):
        a_copies.append(pltpu.make_async_copy(
            a_hbm.at[pl.ds(chunk * 128, 128)], a_ref.at[pl.ds(q * 128, 128)], in_sems.at[TILES + q]
        ))
        a_copies[-1].start()
        if q == 3:
            load_tile(0).start()
    for j in range(1, TILES):
        load_tile(j).start()
    barrier = pltpu.get_barrier_semaphore()
    for peer in peers:
        pl.semaphore_signal(barrier, inc=1, device_id=peer, device_id_type=pl.DeviceIdType.MESH)

    def logits_part(part):
        tiles = (2 * part, 2 * part + 1)
        lanes = slice(part * 512, (part + 1) * 512)
        for copy in a_copies[4 * part:4 * part + 4]:
            copy.wait()
        al_hi[lanes, :], al_lo[lanes, :] = split(a_ref[lanes, :] * (SCALE * LOG2E))
        if part == 1:
            as_hi[...], as_lo[...] = split(a_ref[...] * SCALE)

        for j in range(TILES):
            rows = slice(j * TILE, (j + 1) * TILE)
            if part == 0:
                load_tile(j).wait()
                block = c_ref[rows, :]
                ch, cl = split(block)
                c_hi[rows, :], c_lo[rows, :] = ch, cl
                th, tl = split((block * SCALE).T)
                ct_hi[j], ct_lo[j] = th, tl
            else:
                ch, cl = c_hi[rows, :], c_lo[rows, :]
            left = jnp.concatenate([ch, cl, ch], axis=1)
            first = z * CANDS + j * TILE
            for i in tiles:
                lanes = slice(i * 256, (i + 1) * 256)
                ah, al = al_hi[lanes, :], al_lo[lanes, :]
                logits = dot_nt(left, jnp.concatenate([ah, ah, al], axis=1))
                place = jnp.concatenate([pos_ref[CHUNKS[2 * i]], pos_ref[CHUNKS[2 * i + 1]]], axis=1)
                hit = iota == place - first
                top = jnp.max(logits, axis=0, keepdims=True)
                stat[j, 2:3, lanes] = jnp.sum(jnp.where(hit, logits, 0.0), axis=0, keepdims=True)
                prob = jnp.exp2(logits - top)
                stat[j, 0:1, lanes] = top
                stat[j, 1:2, lanes] = jnp.sum(prob, axis=0, keepdims=True)
                p_ref[2 * i, rows, :] = prob[:, :128]
                p_ref[2 * i + 1, rows, :] = prob[:, 128:]

    def send_stats(part):
        lo, hi = 4 * part, 4 * part + 4
        lanes = slice(lo * 128, hi * 128)
        tops = [stat[j, 0:1, lanes] for j in range(TILES)]
        top = tops[0]
        for j in range(1, TILES):
            top = jnp.maximum(top, tops[j])
        total = jnp.zeros_like(top)
        chosen = jnp.zeros_like(top)
        for j in range(TILES):
            total += stat[j, 1:2, lanes] * jnp.exp2(tops[j] - top)
            chosen += stat[j, 2:3, lanes]
        for k in range(hi - lo):
            piece = slice(k * 128, (k + 1) * 128)
            stat_rx[part, z, 0, k:k + 1, :] = top[:, piece]
            stat_rx[part, z, 1, k:k + 1, :] = total[:, piece]
            stat_rx[part, z, 2, k:k + 1, :] = chosen[:, piece]
        mine = stat_rx.at[part, z]
        return [copies.start(mine, mine, at(dz=d)) for d in (4, 3, 5, 2, 6, 1, 7)]

    def take_stats(part, sent):
        for copy in sent:
            copy.wait_recv()
        lo, hi = 4 * part, 4 * part + 4
        used = slice(0, hi - lo)
        top = stat_rx[part, 0, 0, used, :]
        for k in range(1, 8):
            top = jnp.maximum(top, stat_rx[part, k, 0, used, :])
        total = jnp.zeros_like(top)
        chosen = jnp.zeros_like(top)
        for k in range(8):
            total += stat_rx[part, k, 1, used, :] * jnp.exp2(stat_rx[part, k, 0, used, :] - top)
            chosen += stat_rx[part, k, 2, used, :]
        lse = top + jnp.log2(total)
        loss_rx[0, core, lo:hi, :] = (lse - chosen) * LN2
        for k in range(lo, hi):
            for j in range(TILES):
                back[k, j] = jnp.exp2(stat[j, 0:1, k * 128:(k + 1) * 128] - lse[k - lo:k - lo + 1, :])

    def weights(q, chunk, rows, count, first, j):
        weight = p_ref[q, rows, :] * back[q, j]
        hit = iota[:count] == pos_ref[chunk] - first
        return split(jnp.where(hit, weight - 1.0, weight))

    def cand_blocks(spot, offsets):
        for n, (dx, dy) in enumerate(offsets):
            start = (lax.rem(x + dx, 4) * 4 + lax.rem(y + dy, 4)) * BLOCK
            rows = pl.ds(pl.multiple_of(start, BLOCK), BLOCK)
            first = z * CANDS + start
            both = [weights(q, CHUNKS[q], rows, BLOCK, first, start // TILE) for q in range(8)]
            wh = jnp.concatenate([w[0] for w in both], axis=1)
            wl = jnp.concatenate([w[1] for w in both], axis=1)
            part = dot(wh, as_hi[...]) + dot(wl, as_hi[...]) + dot(wh, as_lo[...])
            blocks[spot + n, 0] = part[:128, :]
            blocks[spot + n, 1] = part[128:, :]
        return cand_send(spot, len(offsets))

    def cand_send(spot, count):
        held = slice(spot, spot + count)
        return copies.start(blocks.at[held, 1 - core], pair_rx.at[held], at(other=True))

    odd = lax.rem(z, 2)

    def offset(part, k):
        return (odd if part == 0 else 1 - odd) + 2 * k

    def anchor_pair(part, pair):
        places = [lax.rem(z + offset(part, k), 8) for k in pair]
        acc = None
        for j in range(TILES):
            rows = slice(j * TILE, (j + 1) * TILE)
            both = [
                weights(4 * part + p // 2, p, rows, TILE, z * CANDS + j * TILE, j) for p in places
            ]
            wh = jnp.concatenate([w[0] for w in both], axis=1)
            wl = jnp.concatenate([w[1] for w in both], axis=1)
            product = dot(ct_hi[j], wh) + dot(ct_lo[j], wh) + dot(ct_hi[j], wl)
            acc = product if acc is None else acc + product
        for n, k in enumerate(pair):
            grad[4 * part + k] = acc[:, n * 128:(n + 1) * 128]
            copy = grad_copy(part, k)
            if k == 0:
                pl.when(odd == 1 - part)(copy.start)
            else:
                copy.start()

    def grad_copy(part, k):
        away = offset(part, k)
        return pltpu.make_async_remote_copy(
            src_ref=grad.at[4 * part + k],
            dst_ref=z_rx.at[away],
            send_sem=z_send.at[4 * part + k if k else 0],
            recv_sem=z_recv.at[away],
            device_id=(anc, lax.rem(z + away, 8)),
            device_id_type=pl.DeviceIdType.MESH,
        )

    def paired(spot):
        return blocks[spot, core] + pair_rx[spot]

    def far_send(i):
        pairs[i].wait_recv()
        for k in range(3):
            both = paired(3 * i + k)
            q0[i, k] = both[:, :128]
            q1[i, k] = both[:, 128:]
        sent = [copies.start(q0.at[i], rx0.at[i], at(dx=AWAY[i]))]
        return sent + [copies.start(q1.at[i, k], ry1.at[i, k], at(dy=AWAY[k])) for k in range(3)]

    logits_part(0)
    pl.semaphore_wait(barrier, len(peers))
    stats0 = send_stats(0)
    logits_part(1)
    stats1 = send_stats(1)
    take_stats(0, stats0)
    anchor_pair(0, (2, 1))
    anchor_pair(0, (3, 0))
    take_stats(1, stats1)
    loss_copies = [copies.start(loss_rx.at[0, core], loss_rx.at[0, core], at(other=True))]
    pairs = [cand_blocks(0, [(AWAY[0], dy) for dy in AWAY])]
    pairs.append(cand_blocks(3, [(AWAY[1], dy) for dy in AWAY]))
    far = far_send(0)
    for copy in loss_copies:
        copy.wait_recv()
    loss_rx[1, x] = loss_rx[0, 0] + loss_rx[0, 1]
    loss_copies = [copies.start(loss_rx.at[1, x], loss_rx.at[1, x], at(dx=d)) for d in AWAY]
    pairs.append(cand_blocks(6, [(AWAY[2], dy) for dy in AWAY]))
    far += far_send(1)

    anchor_pair(1, (2, 1))
    far += far_send(2)
    for copy in loss_copies:
        copy.wait_recv()
    loss_rx[2, y] = (loss_rx[1, 0] + loss_rx[1, 1]) + (loss_rx[1, 2] + loss_rx[1, 3])
    loss_copies = [copies.start(loss_rx.at[2, y], loss_rx.at[2, y], at(dy=d)) for d in AWAY]
    pairs.append(cand_blocks(9, [(0, dy) for dy in AWAY]))
    pairs.append(cand_blocks(12, [(dx, 0) for dx in AWAY]))

    anchor_pair(1, (3, 0))
    last = []
    pairs[3].wait_recv()
    pairs[4].wait_recv()
    for k, d in enumerate(AWAY):
        mine = paired(9 + k)
        qa[k, 0], qa[k, 1] = mine[:, :128], mine[:, 128:]
        last.append(copies.start(qa.at[k, 1], from_y.at[k, 1], at(dy=d)))
        mine = paired(12 + k)
        qb[k, 0], qb[k, 1] = mine[:, :128], mine[:, 128:]
        last.append(copies.start(qb.at[k, 0], from_x.at[k, 0], at(dx=d)))

    pairs.append(cand_blocks(15, [(0, 0)]))
    for copy in far:
        copy.wait_recv()
    for k, d in enumerate(AWAY):
        qa[k, 0] = qa[k, 0] + (rx0[0, k] + rx0[1, k] + rx0[2, k])
        last.append(copies.start(qa.at[k, 0], from_y.at[k, 0], at(dy=d)))
        qb[k, 1] = qb[k, 1] + (ry1[k, 0] + ry1[k, 1] + ry1[k, 2])
        last.append(copies.start(qb.at[k, 1], from_x.at[k, 1], at(dx=d)))

    for copy in loss_copies:
        copy.wait_recv()
    losses = (loss_rx[2, 0] + loss_rx[2, 1]) + (loss_rx[2, 2] + loss_rx[2, 3])
    loss_ref[...] = jnp.sum(losses, keepdims=True) * (1.0 / (32 * ANCHORS))
    for away in range(1, 8):
        pltpu.make_async_remote_copy(
            src_ref=grad.at[away],
            dst_ref=z_rx.at[away],
            send_sem=z_send.at[away],
            recv_sem=z_recv.at[away],
            device_id=at(dz=1),
            device_id_type=pl.DeviceIdType.MESH,
        ).wait_recv()
    near = (z_rx[1] + z_rx[2]) + (z_rx[6] + z_rx[7])
    agrad_ref[...] = (grad[4 * odd] + near + (z_rx[3] + z_rx[4]) + z_rx[5]).T
    pairs[5].wait_recv()
    for copy in last:
        copy.wait_recv()
    own = paired(15)
    for h in range(2):
        lanes = slice(h * 128, (h + 1) * 128)
        cgrad_ref[:, lanes] = own[:, lanes] + (
            (from_y[0, h] + from_y[1, h] + from_y[2, h]) + (from_x[0, h] + from_x[1, h] + from_x[2, h])
        )
    for copy in copies.made:
        copy.wait_send()
    for part, k in ((0, 0), (0, 1), (0, 2), (0, 3), (1, 1), (1, 2), (1, 3)):
        grad_copy(part, k).wait_send()


def body(anchors, candidates, positives):
    vmem = pl.BlockSpec(memory_space=pltpu.VMEM)
    hbm = pl.BlockSpec(memory_space=pl.ANY)
    sems = 64
    grads = [jax.ShapeDtypeStruct((128, WIDTH), F32)] * 2
    loss, anchor_grad, cand_grad = pl.pallas_call(
        kernel,
        out_shape=[jax.ShapeDtypeStruct((1, 1), F32)] + grads,
        in_specs=[hbm, hbm, vmem],
        out_specs=[vmem] * 3,
        scratch_shapes=[
            pltpu.VMEM((ANCHORS, WIDTH), F32),
            pltpu.VMEM((CANDS, WIDTH), F32),
            pltpu.VMEM((CANDS, WIDTH), BF16),
            pltpu.VMEM((CANDS, WIDTH), BF16),
            pltpu.VMEM((TILES, WIDTH, TILE), BF16),
            pltpu.VMEM((TILES, WIDTH, TILE), BF16),
            pltpu.VMEM((ANCHORS, WIDTH), BF16),
            pltpu.VMEM((ANCHORS, WIDTH), BF16),
            pltpu.VMEM((ANCHORS, WIDTH), BF16),
            pltpu.VMEM((ANCHORS, WIDTH), BF16),
            pltpu.VMEM((8, CANDS, 128), F32),
            pltpu.VMEM((TILES, 8, ANCHORS), F32),
            pltpu.VMEM((8, TILES, 1, 128), F32),
            pltpu.VMEM((2, 8, 3, 8, 128), F32),
            pltpu.VMEM((3, 4, 8, 128), F32),
            pltpu.VMEM((16, 2, 128, WIDTH), F32),
            pltpu.VMEM((16, 128, WIDTH), F32),
            pltpu.VMEM((3, 3, 128, 128), F32),
            pltpu.VMEM((3, 3, 128, 128), F32),
            pltpu.VMEM((3, 2, 128, 128), F32),
            pltpu.VMEM((3, 2, 128, 128), F32),
            pltpu.VMEM((3, 3, 128, 128), F32),
            pltpu.VMEM((3, 3, 128, 128), F32),
            pltpu.VMEM((3, 2, 128, 128), F32),
            pltpu.VMEM((3, 2, 128, 128), F32),
            pltpu.VMEM((8, WIDTH, 128), F32),
            pltpu.VMEM((8, WIDTH, 128), F32),
            pltpu.SemaphoreType.DMA((8,)),
            pltpu.SemaphoreType.DMA((8,)),
            pltpu.SemaphoreType.DMA((TILES + 8,)),
            pltpu.SemaphoreType.DMA((sems,)),
            pltpu.SemaphoreType.DMA((sems,)),
        ],
        compiler_params=pltpu.CompilerParams(
            collective_id=0, has_side_effects=True, vmem_limit_bytes=63 << 20
        ),
    )(anchors, candidates, positives.reshape(8, 1, 128))
    return (loss.reshape(()), anchor_grad, cand_grad[None])


def solution(mesh):
    in_specs = (P("anc", None), P("cand", None), P("anc"))
    out_specs = (P(), P(("anc", "cand"), None), P("cand", "anc", None))
    return jax.shard_map(body, mesh=mesh, in_specs=in_specs, out_specs=out_specs, check_vma=False)
```

```python
import math

import jax
import jax.numpy as jnp
from jax import lax
from jax.experimental import pallas as pl
from jax.experimental.pallas import tpu as pltpu
from jax.sharding import PartitionSpec as P

F32 = jnp.float32
BF16 = jnp.bfloat16
WIDTH = 256
ANCHORS = 1024
CANDS = 4096
TILE = 512
TILES = CANDS // TILE
LOG2E = math.log2(math.e)
LN2 = math.log(2.0)
SCALE = 0.25 / math.sqrt(WIDTH)
BLOCK = 256
CHUNKS = (0, 2, 4, 6, 1, 3, 5, 7)
AWAY = (2, 1, 3)


def split(value):
    high = value.astype(BF16)
    return high, (value - high.astype(F32)).astype(BF16)


def dot(left, right):
    return jnp.dot(left, right, preferred_element_type=F32)


def dot_nt(left, right):
    return lax.dot_general(left, right, (((1,), (1,)), ((), ())), preferred_element_type=F32)


class Copies:
    def __init__(self, send_sems, recv_sems):
        self.send_sems, self.recv_sems = send_sems, recv_sems
        self.made = []

    def start(self, source, target, device):
        index = len(self.made)
        copy = pltpu.make_async_remote_copy(
            src_ref=source,
            dst_ref=target,
            send_sem=self.send_sems.at[index],
            recv_sem=self.recv_sems.at[index],
            device_id=device,
            device_id_type=pl.DeviceIdType.MESH,
        )
        copy.start()
        self.made.append(copy)
        return copy


def kernel(
    a_hbm, c_hbm, pos_ref, loss_ref, near_ref, far_ref,
    a_ref, c_ref, c_hi, c_lo, ct_hi, ct_lo, al_hi, al_lo, as_hi, as_lo,
    p_ref, stat, back, stat_rx, loss_rx,
    blocks, pair_rx, q0, q1, qa, qb, rx0, ry1, from_y, from_x, grad, z_rx, z_send, z_recv,
    in_sems, send_sems, recv_sems,
):
    anc = lax.axis_index("anc")
    z = lax.axis_index("cand")
    x, y, core = anc // 8, lax.rem(anc // 2, 4), lax.rem(anc, 2)

    def at(dx=0, dy=0, other=False, dz=0):
        px = lax.rem(x + dx, 4)
        py = lax.rem(y + dy, 4)
        pc = 1 - core if other else core
        return ((px * 4 + py) * 2 + pc, lax.rem(z + dz, 8))

    peers = [at(other=True)]
    peers += [at(dx=d) for d in (1, 2, 3)] + [at(dy=d) for d in (1, 2, 3)]
    peers += [at(dz=d) for d in range(1, 8)]
    copies = Copies(send_sems, recv_sems)
    iota = lax.broadcasted_iota(jnp.int32, (TILE, 1), 0)

    def load_tile(j):
        rows = pl.ds(pl.multiple_of(j * TILE, TILE), TILE)
        return pltpu.make_async_copy(c_hbm.at[rows], c_ref.at[rows], in_sems.at[j])

    a_copies = []
    for q, chunk in enumerate(CHUNKS):
        a_copies.append(pltpu.make_async_copy(
            a_hbm.at[pl.ds(chunk * 128, 128)], a_ref.at[pl.ds(q * 128, 128)], in_sems.at[TILES + q]
        ))
        a_copies[-1].start()
        if q == 3:
            load_tile(0).start()
    for j in range(1, TILES):
        load_tile(j).start()
    barrier = pltpu.get_barrier_semaphore()
    for peer in peers:
        pl.semaphore_signal(barrier, inc=1, device_id=peer, device_id_type=pl.DeviceIdType.MESH)

    def logits_part(part):
        tiles = (2 * part, 2 * part + 1)
        lanes = slice(part * 512, (part + 1) * 512)
        for copy in a_copies[4 * part:4 * part + 4]:
            copy.wait()
        al_hi[lanes, :], al_lo[lanes, :] = split(a_ref[lanes, :] * (SCALE * LOG2E))
        if part == 1:
            as_hi[...], as_lo[...] = split(a_ref[...] * SCALE)

        @pl.loop(0, TILES // 2)
        def _(step):
            for sub in range(2):
                j = step * 2 + sub
                rows = pl.ds(pl.multiple_of(j * TILE, TILE), TILE)
                if part == 0:
                    load_tile(j).wait()
                    block = c_ref[rows, :]
                    ch, cl = split(block)
                    c_hi[rows, :], c_lo[rows, :] = ch, cl
                    th, tl = split((block * SCALE).T)
                    ct_hi[j], ct_lo[j] = th, tl
                else:
                    ch, cl = c_hi[rows, :], c_lo[rows, :]
                left = jnp.concatenate([ch, cl, ch], axis=1)
                first = z * CANDS + j * TILE
                for i in tiles:
                    lanes = slice(i * 256, (i + 1) * 256)
                    ah, al = al_hi[lanes, :], al_lo[lanes, :]
                    logits = dot_nt(left, jnp.concatenate([ah, ah, al], axis=1))
                    place = jnp.concatenate([pos_ref[CHUNKS[2 * i]], pos_ref[CHUNKS[2 * i + 1]]], axis=1)
                    hit = iota == place - first
                    top = jnp.max(logits, axis=0, keepdims=True)
                    stat[j, 2:3, lanes] = jnp.sum(jnp.where(hit, logits, 0.0), axis=0, keepdims=True)
                    prob = jnp.exp2(logits - top)
                    stat[j, 0:1, lanes] = top
                    stat[j, 1:2, lanes] = jnp.sum(prob, axis=0, keepdims=True)
                    p_ref[2 * i, rows, :] = prob[:, :128]
                    p_ref[2 * i + 1, rows, :] = prob[:, 128:]

    def send_stats(part):
        lo, hi = 4 * part, 4 * part + 4
        lanes = slice(lo * 128, hi * 128)
        tops = [stat[j, 0:1, lanes] for j in range(TILES)]
        top = tops[0]
        for j in range(1, TILES):
            top = jnp.maximum(top, tops[j])
        total = jnp.zeros_like(top)
        chosen = jnp.zeros_like(top)
        for j in range(TILES):
            total += stat[j, 1:2, lanes] * jnp.exp2(tops[j] - top)
            chosen += stat[j, 2:3, lanes]
        for k in range(hi - lo):
            piece = slice(k * 128, (k + 1) * 128)
            stat_rx[part, z, 0, k:k + 1, :] = top[:, piece]
            stat_rx[part, z, 1, k:k + 1, :] = total[:, piece]
            stat_rx[part, z, 2, k:k + 1, :] = chosen[:, piece]
        mine = stat_rx.at[part, z]
        return [copies.start(mine, mine, at(dz=d)) for d in (4, 3, 5, 2, 6, 1, 7)]

    def take_stats(part, sent):
        for copy in sent:
            copy.wait_recv()
        lo, hi = 4 * part, 4 * part + 4
        used = slice(0, hi - lo)
        top = stat_rx[part, 0, 0, used, :]
        for k in range(1, 8):
            top = jnp.maximum(top, stat_rx[part, k, 0, used, :])
        total = jnp.zeros_like(top)
        chosen = jnp.zeros_like(top)
        for k in range(8):
            total += stat_rx[part, k, 1, used, :] * jnp.exp2(stat_rx[part, k, 0, used, :] - top)
            chosen += stat_rx[part, k, 2, used, :]
        lse = top + jnp.log2(total)
        loss_rx[0, core, lo:hi, :] = (lse - chosen) * LN2
        for k in range(lo, hi):
            for j in range(TILES):
                back[k, j] = jnp.exp2(stat[j, 0:1, k * 128:(k + 1) * 128] - lse[k - lo:k - lo + 1, :])

    def weights(q, chunk, rows, count, first, j):
        weight = p_ref[q, rows, :] * back[q, j]
        hit = iota[:count] == pos_ref[chunk] - first
        return split(jnp.where(hit, weight - 1.0, weight))

    def cand_blocks(spot, offsets):
        for n, (dx, dy) in enumerate(offsets):
            start = (lax.rem(x + dx, 4) * 4 + lax.rem(y + dy, 4)) * BLOCK
            rows = pl.ds(pl.multiple_of(start, BLOCK), BLOCK)
            first = z * CANDS + start
            both = [weights(q, CHUNKS[q], rows, BLOCK, first, start // TILE) for q in range(8)]
            wh = jnp.concatenate([w[0] for w in both], axis=1)
            wl = jnp.concatenate([w[1] for w in both], axis=1)
            part = dot(wh, as_hi[...]) + dot(wl, as_hi[...]) + dot(wh, as_lo[...])
            blocks[spot + n, 0] = part[:128, :]
            blocks[spot + n, 1] = part[128:, :]
        return cand_send(spot, len(offsets))

    def cand_send(spot, count):
        held = slice(spot, spot + count)
        return copies.start(blocks.at[held, 1 - core], pair_rx.at[held], at(other=True))

    odd = lax.rem(z, 2)

    def offset(part, k):
        return (odd if part == 0 else 1 - odd) + 2 * k

    def anchor_pair(part, pair):
        places = [lax.rem(z + offset(part, k), 8) for k in pair]
        acc = None
        for j in range(TILES):
            rows = slice(j * TILE, (j + 1) * TILE)
            both = [
                weights(4 * part + p // 2, p, rows, TILE, z * CANDS + j * TILE, j) for p in places
            ]
            wh = jnp.concatenate([w[0] for w in both], axis=1)
            wl = jnp.concatenate([w[1] for w in both], axis=1)
            product = dot(ct_hi[j], wh) + dot(ct_lo[j], wh) + dot(ct_hi[j], wl)
            acc = product if acc is None else acc + product
        for n, k in enumerate(pair):
            grad[4 * part + k] = acc[:, n * 128:(n + 1) * 128]
            copy = grad_copy(part, k)
            if k == 0:
                pl.when(odd == 1 - part)(copy.start)
            else:
                copy.start()

    def grad_copy(part, k):
        away = offset(part, k)
        return pltpu.make_async_remote_copy(
            src_ref=grad.at[4 * part + k],
            dst_ref=z_rx.at[away],
            send_sem=z_send.at[4 * part + k if k else 0],
            recv_sem=z_recv.at[away],
            device_id=(anc, lax.rem(z + away, 8)),
            device_id_type=pl.DeviceIdType.MESH,
        )

    def paired(spot):
        return blocks[spot, core] + pair_rx[spot]

    def far_send(i):
        pairs[i].wait_recv()
        for k in range(3):
            both = paired(3 * i + k)
            q0[i, k] = both[:, :128]
            q1[i, k] = both[:, 128:]
        sent = [copies.start(q0.at[i], rx0.at[i], at(dx=AWAY[i]))]
        return sent + [copies.start(q1.at[i, k], ry1.at[i, k], at(dy=AWAY[k])) for k in range(3)]

    logits_part(0)
    pl.semaphore_wait(barrier, len(peers))
    stats0 = send_stats(0)
    logits_part(1)
    stats1 = send_stats(1)
    take_stats(0, stats0)
    anchor_pair(0, (2, 1))
    anchor_pair(0, (3, 0))
    take_stats(1, stats1)
    loss_copies = [copies.start(loss_rx.at[0, core], loss_rx.at[0, core], at(other=True))]
    pairs = [cand_blocks(0, [(AWAY[0], dy) for dy in AWAY])]
    pairs.append(cand_blocks(3, [(AWAY[1], dy) for dy in AWAY]))
    far = far_send(0)
    for copy in loss_copies:
        copy.wait_recv()
    loss_rx[1, x] = loss_rx[0, 0] + loss_rx[0, 1]
    loss_copies = [copies.start(loss_rx.at[1, x], loss_rx.at[1, x], at(dx=d)) for d in AWAY]
    pairs.append(cand_blocks(6, [(AWAY[2], dy) for dy in AWAY]))
    far += far_send(1)

    anchor_pair(1, (2, 1))
    far += far_send(2)
    for copy in loss_copies:
        copy.wait_recv()
    loss_rx[2, y] = (loss_rx[1, 0] + loss_rx[1, 1]) + (loss_rx[1, 2] + loss_rx[1, 3])
    loss_copies = [copies.start(loss_rx.at[2, y], loss_rx.at[2, y], at(dy=d)) for d in AWAY]
    pairs.append(cand_blocks(9, [(0, dy) for dy in AWAY]))
    pairs.append(cand_blocks(12, [(dx, 0) for dx in AWAY]))

    anchor_pair(1, (3, 0))
    last = []
    pairs[3].wait_recv()
    pairs[4].wait_recv()
    for k, d in enumerate(AWAY):
        mine = paired(9 + k)
        qa[k, 0], qa[k, 1] = mine[:, :128], mine[:, 128:]
        last.append(copies.start(qa.at[k, 1], from_y.at[k, 1], at(dy=d)))
        mine = paired(12 + k)
        qb[k, 0], qb[k, 1] = mine[:, :128], mine[:, 128:]
        last.append(copies.start(qb.at[k, 0], from_x.at[k, 0], at(dx=d)))

    pairs.append(cand_blocks(15, [(0, 0)]))
    for copy in far:
        copy.wait_recv()
    for k, d in enumerate(AWAY):
        qa[k, 0] = qa[k, 0] + (rx0[0, k] + rx0[1, k] + rx0[2, k])
        last.append(copies.start(qa.at[k, 0], from_y.at[k, 0], at(dy=d)))
        qb[k, 1] = qb[k, 1] + (ry1[k, 0] + ry1[k, 1] + ry1[k, 2])
        last.append(copies.start(qb.at[k, 1], from_x.at[k, 1], at(dx=d)))

    for copy in loss_copies:
        copy.wait_recv()
    losses = (loss_rx[2, 0] + loss_rx[2, 1]) + (loss_rx[2, 2] + loss_rx[2, 3])
    loss_ref[...] = jnp.sum(losses, keepdims=True) * (1.0 / (32 * ANCHORS))
    for away in range(1, 8):
        pltpu.make_async_remote_copy(
            src_ref=grad.at[away],
            dst_ref=z_rx.at[away],
            send_sem=z_send.at[away],
            recv_sem=z_recv.at[away],
            device_id=at(dz=1),
            device_id_type=pl.DeviceIdType.MESH,
        ).wait_recv()
    near_ref[0] = (grad[4 * odd] + (z_rx[1] + z_rx[2])).T
    far_ref[0] = ((z_rx[6] + z_rx[7]) + (z_rx[3] + z_rx[4]) + z_rx[5]).T
    pairs[5].wait_recv()
    for copy in last:
        copy.wait_recv()
    own = paired(15)
    for h in range(2):
        lanes = slice(h * 128, (h + 1) * 128)
        near_ref[1, :, lanes] = own[:, lanes] + (from_y[0, h] + from_y[1, h] + from_y[2, h])
        far_ref[1, :, lanes] = from_x[0, h] + from_x[1, h] + from_x[2, h]
    for copy in copies.made:
        copy.wait_send()
    for part, k in ((0, 0), (0, 1), (0, 2), (0, 3), (1, 1), (1, 2), (1, 3)):
        grad_copy(part, k).wait_send()


def body(anchors, candidates, positives):
    vmem = pl.BlockSpec(memory_space=pltpu.VMEM)
    hbm = pl.BlockSpec(memory_space=pl.ANY)
    sems = 64
    grads = [jax.ShapeDtypeStruct((2, 128, WIDTH), F32)] * 2
    loss, near, far = pl.pallas_call(
        kernel,
        out_shape=[jax.ShapeDtypeStruct((1, 1), F32)] + grads,
        in_specs=[hbm, hbm, vmem],
        out_specs=[vmem] * 3,
        scratch_shapes=[
            pltpu.VMEM((ANCHORS, WIDTH), F32),
            pltpu.VMEM((CANDS, WIDTH), F32),
            pltpu.VMEM((CANDS, WIDTH), BF16),
            pltpu.VMEM((CANDS, WIDTH), BF16),
            pltpu.VMEM((TILES, WIDTH, TILE), BF16),
            pltpu.VMEM((TILES, WIDTH, TILE), BF16),
            pltpu.VMEM((ANCHORS, WIDTH), BF16),
            pltpu.VMEM((ANCHORS, WIDTH), BF16),
            pltpu.VMEM((ANCHORS, WIDTH), BF16),
            pltpu.VMEM((ANCHORS, WIDTH), BF16),
            pltpu.VMEM((8, CANDS, 128), F32),
            pltpu.VMEM((TILES, 8, ANCHORS), F32),
            pltpu.VMEM((8, TILES, 1, 128), F32),
            pltpu.VMEM((2, 8, 3, 8, 128), F32),
            pltpu.VMEM((3, 4, 8, 128), F32),
            pltpu.VMEM((16, 2, 128, WIDTH), F32),
            pltpu.VMEM((16, 128, WIDTH), F32),
            pltpu.VMEM((3, 3, 128, 128), F32),
            pltpu.VMEM((3, 3, 128, 128), F32),
            pltpu.VMEM((3, 2, 128, 128), F32),
            pltpu.VMEM((3, 2, 128, 128), F32),
            pltpu.VMEM((3, 3, 128, 128), F32),
            pltpu.VMEM((3, 3, 128, 128), F32),
            pltpu.VMEM((3, 2, 128, 128), F32),
            pltpu.VMEM((3, 2, 128, 128), F32),
            pltpu.VMEM((8, WIDTH, 128), F32),
            pltpu.VMEM((8, WIDTH, 128), F32),
            pltpu.SemaphoreType.DMA((8,)),
            pltpu.SemaphoreType.DMA((8,)),
            pltpu.SemaphoreType.DMA((TILES + 8,)),
            pltpu.SemaphoreType.DMA((sems,)),
            pltpu.SemaphoreType.DMA((sems,)),
        ],
        compiler_params=pltpu.CompilerParams(
            collective_id=0, has_side_effects=True, vmem_limit_bytes=63 << 20
        ),
    )(anchors, candidates, positives.reshape(8, 1, 128))
    return (loss.reshape(()), near[0] + far[0], near[1:] + far[1:])


def solution(mesh):
    in_specs = (P("anc", None), P("cand", None), P("anc"))
    out_specs = (P(), P(("anc", "cand"), None), P("cand", "anc", None))
    return jax.shard_map(body, mesh=mesh, in_specs=in_specs, out_specs=out_specs, check_vma=False)
```
